256 devices in a mesh: ex: 8 (over z_lo, core), ey: 32 (over z_hi, x, y).
Axes of the slice: x: 4, y: 4, z: 8 (z_hi: 2, z_lo: 4; z = z_hi * 4 + z_lo), core: 2. Of those that a mesh axis runs over, the one named last changes fastest.
Arguments:
- tokens: bfloat16 [256, 256, 1024], P(('ex', 'ey')), may hold values from -16 to 16
- slot_param: bfloat16 [1024, 64], replicated, may hold values from -0.75 to 0.75
- weight_in: bfloat16 [64, 1024, 4096], P('ey', None, 'ex'), may hold values from -0.1875 to 0.1875
- weight_out: bfloat16 [64, 4096, 1024], P('ey', 'ex'), may hold values from -0.09375 to 0.09375
- grad_out: bfloat16 [256, 256, 1024], P(('ex', 'ey')), may hold values from -6 to 6
Outputs:
- grad_tokens: bfloat16 [256, 256, 1024], P(('ex', 'ey'))
- grad_param: float32 [1024, 64], replicated
- grad_win: bfloat16 [64, 1024, 4096], P('ey', None, 'ex')
- grad_wout: bfloat16 [64, 4096, 1024], P('ey', 'ex')
The draws below stay inside these ranges and needn't reach their ends.
All inputs are finite; a program needn't handle non-finite values.
Results may differ from the reference program's by a relative error of at most 0.017.
Values may be sent and summed in bfloat16 or wider, within the bound.
A program may use at most 64 MiB of HBM per device.

```python
import jax
import jax.numpy as jnp
from jax import lax

D = 1024
FF = 4096
PATCHES = 256
EXPERTS = 64
IMAGES = 256


def slot_table(key):
    raw = 0.125 * jax.random.normal(jax.random.fold_in(key, 11), (D, EXPERTS), jnp.float32)
    return jnp.clip(raw, -0.75, 0.75)


def draw_slot_param(key, part):
    return slot_table(key).astype(jnp.bfloat16)


def draw_tokens(key, part):
    shape = (IMAGES, PATCHES, D)
    base = jax.random.normal(jax.random.fold_in(key, 3), shape, jnp.float32)
    return jnp.clip(base, -6.0, 6.0).astype(jnp.bfloat16)


def block_scale(stream_key, dims, shards, low, high):
    gain, own = 1.0, jax.random.fold_in(stream_key, 6)
    for dim, parts in shards:
        steps = jnp.exp(jax.random.uniform(jax.random.fold_in(own, dim), (parts,), jnp.float32, low / len(shards), high / len(shards)))
        gain = gain * jnp.repeat(steps, dims[dim] // parts).reshape([-1 if axis == dim else 1 for axis in range(len(dims))])
    return gain


def centred(key, shape, spread, most, split=(), kind=jnp.bfloat16):
    result = spread * jax.random.normal(key, shape, jnp.float32)
    if split:
        result = result * block_scale(key, shape, split, -0.22, 0.18)
    return jnp.clip(result, -most, most).astype(kind)


def setup_inputs(seed: int = 0) -> dict:
    arg_keys = jax.random.split(jax.random.key(seed), 6)
    tokens = draw_tokens(jax.random.fold_in(arg_keys[5], 71), 0)
    slot_param = draw_slot_param(jax.random.fold_in(arg_keys[5], 71), 0)
    weight_in = centred(arg_keys[2], (EXPERTS, D, FF), D ** -0.5, 0.1875, ((0, 32), (2, 8)))
    weight_out = centred(arg_keys[3], (EXPERTS, FF, D), FF ** -0.5, 0.09375, ((0, 32), (1, 8)))
    grad_out = centred(arg_keys[4], (IMAGES, PATCHES, D), 1.0, 6.0, ((0, 256),))
    return dict(tokens=tokens, slot_param=slot_param, weight_in=weight_in, weight_out=weight_out, grad_out=grad_out)


def gelu_parts(pre):
    cdf = 0.5 * (1.0 + lax.erf(pre * 0.7071067811865476))
    slope = cdf + pre * jnp.exp(-0.5 * pre * pre) * 0.3989422804014327
    return pre * cdf, slope


def softmax_along(values, axis):
    top = jnp.max(values, axis=axis, keepdims=True)
    expo = jnp.exp(values - top)
    return expo / jnp.sum(expo, axis=axis, keepdims=True)


def expert_step(inputs):
    slot_x, slot_g, w_first, w_second = inputs
    pre = jnp.dot(slot_x, w_first, preferred_element_type=jnp.float32)
    value, slope = gelu_parts(pre)
    hidden = value.astype(jnp.bfloat16)
    slot_y = jnp.dot(hidden, w_second, preferred_element_type=jnp.float32).astype(jnp.bfloat16)
    back = jnp.dot(slot_g, w_second.T, preferred_element_type=jnp.float32)
    dpre = (back * slope).astype(jnp.bfloat16)
    grad_x = jnp.dot(dpre, w_first.T, preferred_element_type=jnp.float32).astype(jnp.bfloat16)
    grad_first = jnp.dot(slot_x.T, dpre, preferred_element_type=jnp.float32).astype(jnp.bfloat16)
    grad_second = jnp.dot(hidden.T, slot_g, preferred_element_type=jnp.float32).astype(jnp.bfloat16)
    return slot_y, grad_x, grad_first, grad_second


def reference(tokens, slot_param, weight_in, weight_out, grad_out):
    xf = tokens.astype(jnp.float32)
    gf = grad_out.astype(jnp.float32)
    pf = slot_param.astype(jnp.float32)
    logits = jnp.einsum('bpd,ds->bps', xf, pf)
    dispatch = softmax_along(logits, 1)
    combine = softmax_along(logits, 2)
    dispatch_b = dispatch.astype(jnp.bfloat16)
    combine_b = combine.astype(jnp.bfloat16)
    slot_in = jnp.einsum('bps,bpd->sbd', dispatch_b.astype(jnp.float32), xf).astype(jnp.bfloat16)
    slot_cot = jnp.einsum('bps,bpd->sbd', combine_b.astype(jnp.float32), gf).astype(jnp.bfloat16)
    slot_out, grad_slot, grad_win, grad_wout = lax.map(expert_step, (slot_in, slot_cot, weight_in, weight_out))
    d_combine = jnp.einsum('bpd,sbd->bps', gf, slot_out.astype(jnp.float32))
    d_dispatch = jnp.einsum('bpd,sbd->bps', xf, grad_slot.astype(jnp.float32))
    d_logits = dispatch * (d_dispatch - jnp.sum(dispatch * d_dispatch, axis=1, keepdims=True))
    d_logits = d_logits + combine * (d_combine - jnp.sum(combine * d_combine, axis=2, keepdims=True))
    d_logits = d_logits.astype(jnp.bfloat16).astype(jnp.float32)
    grad_tokens = jnp.einsum('bps,sbd->bpd', dispatch_b.astype(jnp.float32), grad_slot.astype(jnp.float32))
    grad_tokens = (grad_tokens + jnp.einsum('bps,ds->bpd', d_logits, pf)).astype(jnp.bfloat16)
    grad_param = jnp.einsum('bpd,bps->ds', xf, d_logits)
    return grad_tokens, grad_param, grad_win, grad_wout
```

```python
import functools

import jax
import jax.numpy as jnp
from jax import lax
from jax.experimental import pallas as pl
from jax.experimental.pallas import tpu as pltpu
from jax.sharding import Mesh
from jax.sharding import PartitionSpec as P

AXES = ("zl", "core", "zh", "xy")
EX = ("zl", "core")
EY = ("zh", "xy")
ALL = AXES
ZH = 2
LANES = 128
F32 = jnp.float32
BF16 = jnp.bfloat16


def dot(a, b, ca, cb):
    return lax.dot_general(a, b, (((ca,), (cb,)), ((), ())), preferred_element_type=F32)


def softmax_along(values, axis):
    top = jnp.max(values, axis=axis, keepdims=True)
    expo = jnp.exp(values - top)
    return expo / jnp.sum(expo, axis=axis, keepdims=True)


def gelu_parts(pre):
    cdf = 0.5 * (1.0 + lax.erf(pre * 0.7071067811865476))
    slope = cdf + pre * jnp.exp(-0.5 * pre * pre) * 0.3989422804014327
    return (pre * cdf, slope)


def kernel(
    ZL, XY,
    tok_hbm, par_hbm, wi_hbm, wo_hbm, go_hbm,
    gt_hbm, gp_hbm, gwi_hbm, gwo_hbm,
    tok, par, go, wi, wo,
    disp, comb, disp_b, comb_b,
    rows32, send1, recv1, planes, gathered,
    pre_s, back_s, hid, dpre,
    ysend, yrecv, send2, recv2, slots,
    gt_v, gwi_v, gwo_v,
    xsend, xrecv, zsend, zrecv, usend, urecv, gp_v,
    in_sem, out_sem, w_send, w_recv, g_send, g_recv,
    a_send, a_recv, b_send, b_recv, y_send, y_recv, c_send, c_recv,
    x_send, x_recv, z_send, z_recv, u_send, u_recv,
):
    T = 2 * XY
    NZ = ZL * ZH
    D = tok.shape[1]
    J = D // LANES
    PAIR = 2 * J
    zl = lax.axis_index("zl")
    core = lax.axis_index("core")
    zh = lax.axis_index("zh")
    xy = lax.axis_index("xy")
    me_t = xy * 2 + core
    me_z = zh * ZL + zl

    def in_plane(d):
        t = lax.rem(me_t + d, T)
        return t, (zl, lax.rem(t, 2), zh, lax.div(t, 2))

    def along_z(d):
        z = lax.rem(me_z + d, NZ)
        return z, (lax.rem(z, ZL), core, lax.div(z, ZL), xy)

    sibling = (zl, 1 - core, zh, xy)

    def remote(src, dst, send_sem, recv_sem, device):
        return pltpu.make_async_remote_copy(
            src_ref=src, dst_ref=dst, send_sem=send_sem, recv_sem=recv_sem,
            device_id=device, device_id_type=pl.DeviceIdType.MESH,
        )

    barrier = pltpu.get_barrier_semaphore()

    def greet_plane(d, carry):
        pl.semaphore_signal(barrier, inc=1, device_id=in_plane(d)[1], device_id_type=pl.DeviceIdType.MESH)
        return carry

    def greet_z(d, carry):
        pl.semaphore_signal(barrier, inc=1, device_id=along_z(d)[1], device_id_type=pl.DeviceIdType.MESH)
        return carry

    loads = [
        pltpu.make_async_copy(tok_hbm, tok, in_sem.at[0]),
        pltpu.make_async_copy(par_hbm, par, in_sem.at[1]),
        pltpu.make_async_copy(go_hbm, go, in_sem.at[2]),
        pltpu.make_async_copy(wi_hbm.at[core], wi.at[core], in_sem.at[3]),
        pltpu.make_async_copy(wo_hbm.at[core], wo.at[core], in_sem.at[4]),
    ]
    for load in loads:
        load.start()
    lax.fori_loop(1, T, greet_plane, 0)
    lax.fori_loop(1, NZ, greet_z, 0)

    def pack(part, h, w):
        for j in range(J):
            rows32[pl.ds(h * PAIR + w * J + j, T, stride=ZH * PAIR), :] = part[:, j * LANES : (j + 1) * LANES]

    def unpack(h, w, j):
        return rows32[pl.ds(h * PAIR + w * J + j, T, stride=ZH * PAIR), :].astype(BF16)

    def all_to_all(send, recv, send_sem, recv_sem):
        def go_to(d, carry):
            t, device = in_plane(d)
            remote(send.at[t], recv.at[me_t], send_sem, recv_sem, device).start()
            return carry

        lax.fori_loop(1, T, go_to, 0)

    def wait_all(ref, count, sem):
        part = ref.at[pl.ds(0, count)]
        pltpu.make_async_copy(part, part, sem).wait()

    loads[0].wait()
    loads[1].wait()
    logits = dot(tok[...], par[...], 1, 0)
    dispatch = softmax_along(logits, 0)
    combine = softmax_along(logits, 1)
    disp[...] = dispatch
    comb[...] = combine
    disp_b[...] = dispatch.astype(BF16)
    comb_b[...] = combine.astype(BF16)
    slot_in = dot(disp_b[...], tok[...], 0, 0)
    for h in range(ZH):
        pack(slot_in[h * T : (h + 1) * T], h, 0)
    loads[2].wait()
    slot_cot = dot(comb_b[...], go[...], 0, 0)
    for h in range(ZH):
        pack(slot_cot[h * T : (h + 1) * T], h, 1)
    send1[...] = rows32[...].astype(BF16).reshape(send1.shape)

    pl.semaphore_wait(barrier, T - 1 + NZ - 1)
    all_to_all(send1, recv1, a_send, a_recv)
    swap = [
        remote(wi_hbm.at[1 - core], wi.at[core], w_send.at[0], w_recv.at[0], sibling),
        remote(wo_hbm.at[1 - core], wo.at[core], w_send.at[1], w_recv.at[1], sibling),
    ]
    for copy in swap:
        copy.start()
    wait_all(send1, T - 1, a_send)
    wait_all(recv1, T - 1, a_recv)
    recv1[me_t] = send1[me_t]
    rows32[...] = recv1[...].reshape(rows32.shape).astype(F32)
    for h in range(ZH):
        for w in range(2):
            for j in range(J):
                planes[h, w, :, j * LANES : (j + 1) * LANES] = unpack(h, w, j)

    def send_plane(d, carry):
        z, device = along_z(d)
        remote(planes.at[lax.div(z, ZL)], gathered.at[me_z], b_send.at[z], b_recv.at[me_z], device).start()
        return carry

    def wait_plane(d, carry):
        z, device = along_z(d)
        remote(planes.at[0], gathered.at[z], b_send.at[z], b_recv.at[z], device).wait()
        return carry

    lax.fori_loop(1, NZ, send_plane, 0)
    gathered[me_z] = planes[zh]
    for copy in loads[3:] + swap:
        copy.wait()
    lax.fori_loop(1, NZ, wait_plane, 0)

    rows = NZ * T
    slot_x = gathered[:, 0].reshape(rows, D)
    slot_g = gathered[:, 1].reshape(rows, D)
    step = min(16, rows)
    for f in range(2):
        pre_s[...] = dot(slot_x, wi[f], 1, 0)
        back_s[...] = dot(slot_g, wo[f], 1, 1)

        def activate(k, carry):
            part = pl.ds(pl.multiple_of(k * step, step), step)
            value, slope = gelu_parts(pre_s[part, :])
            hid[f, part, :] = value.astype(BF16)
            dpre[f, part, :] = (back_s[part, :] * slope).astype(BF16)
            return carry

        lax.fori_loop(0, rows // step, activate, 0)
    ysend[:, 0] = (dot(hid[0], wo[0], 1, 0) + dot(hid[1], wo[1], 1, 0)).astype(BF16).reshape(NZ, T, D)
    ysend[:, 1] = (dot(dpre[0], wi[0], 1, 1) + dot(dpre[1], wi[1], 1, 1)).astype(BF16).reshape(NZ, T, D)

    def send_back(d, carry):
        z, device = along_z(d)
        remote(ysend.at[z], yrecv.at[me_z], y_send.at[z], y_recv.at[me_z], device).start()
        return carry

    def wait_back(d, carry):
        z, device = along_z(d)
        remote(ysend.at[z], yrecv.at[z], y_send.at[z], y_recv.at[z], device).wait()
        return carry

    lax.fori_loop(1, NZ, send_back, 0)
    yrecv[me_z] = ysend[me_z]
    for f in range(2):
        gwi_v[f] = dot(slot_x, dpre[f], 0, 0).astype(BF16)
        gwo_v[f] = dot(hid[f], slot_g, 0, 0).astype(BF16)
    stores = [
        pltpu.make_async_copy(gwi_v.at[core], gwi_hbm.at[core], out_sem.at[0]),
        pltpu.make_async_copy(gwo_v.at[core], gwo_hbm.at[core], out_sem.at[1]),
        remote(gwi_v.at[1 - core], gwi_hbm.at[core], g_send.at[0], g_recv.at[0], sibling),
        remote(gwo_v.at[1 - core], gwo_hbm.at[core], g_send.at[1], g_recv.at[1], sibling),
    ]
    for copy in stores:
        copy.start()
    lax.fori_loop(1, NZ, wait_back, 0)
    for h in range(ZH):
        for w in range(2):
            total = yrecv[h * ZL, w].astype(F32)
            for k in range(1, ZL):
                total = total + yrecv[h * ZL + k, w].astype(F32)
            pack(total, h, w)
    send2[...] = rows32[...].astype(BF16).reshape(send2.shape)
    all_to_all(send2, recv2, c_send, c_recv)
    wait_all(send2, T - 1, c_send)
    wait_all(recv2, T - 1, c_recv)
    recv2[me_t] = send2[me_t]
    rows32[...] = recv2[...].reshape(rows32.shape).astype(F32)
    for h in range(ZH):
        for w in range(2):
            for j in range(J):
                slots[w, h * T : (h + 1) * T, j * LANES : (j + 1) * LANES] = unpack(h, w, j)

    d_combine = dot(go[...], slots[0], 1, 1)
    d_dispatch = dot(tok[...], slots[1], 1, 1)
    dispatch = disp[...]
    combine = comb[...]
    d_logits = dispatch * (d_dispatch - jnp.sum(dispatch * d_dispatch, axis=0, keepdims=True))
    d_logits = d_logits + combine * (d_combine - jnp.sum(combine * d_combine, axis=1, keepdims=True))
    logit_grad = d_logits.astype(BF16)
    local_param = dot(logit_grad, tok[...], 0, 0)

    S = disp.shape[1]
    for r in range(S // 8):
        for j in range(J):
            k = r * J + j
            xsend[k // 2, k % 2] = local_param[r * 8 : (r + 1) * 8, j * LANES : (j + 1) * LANES]
    all_to_all(xsend, xrecv, x_send, x_recv)
    gt_v[...] = (dot(disp_b[...], slots[1], 1, 0) + dot(logit_grad, par[...], 1, 1)).astype(BF16)
    store_gt = pltpu.make_async_copy(gt_v, gt_hbm, out_sem.at[2])
    store_gt.start()
    wait_all(xsend, T - 1, x_send)
    wait_all(xrecv, T - 1, x_recv)
    xrecv[me_t] = xsend[me_t]
    zsend[...] = jnp.sum(xrecv[...], axis=0)

    def send_sum(d, carry):
        z, device = along_z(d)
        remote(zsend, zrecv.at[me_z], z_send, z_recv, device).start()
        return carry

    lax.fori_loop(1, NZ, send_sum, 0)
    wait_all(zrecv, NZ - 1, z_send)
    wait_all(zrecv, NZ - 1, z_recv)
    zrecv[me_z] = zsend[...]
    usend[...] = jnp.sum(zrecv[...], axis=0)

    def send_total(d, carry):
        remote(usend, urecv.at[me_t], u_send, u_recv, in_plane(d)[1]).start()
        return carry

    lax.fori_loop(1, T, send_total, 0)
    wait_all(urecv, T - 1, u_send)
    wait_all(urecv, T - 1, u_recv)
    urecv[me_t] = usend[...]
    for r in range(S // 8):
        for j in range(J):
            k = r * J + j
            gp_v[r * 8 : (r + 1) * 8, j * LANES : (j + 1) * LANES] = urecv[k // 2, k % 2]
    store_gp = pltpu.make_async_copy(gp_v, gp_hbm, out_sem.at[3])
    store_gp.start()
    for copy in stores + [store_gt, store_gp]:
        copy.wait()


def per_device(ZL, XY, tokens, slot_param, weight_in, weight_out, grad_out):
    _, patches, D = tokens.shape
    S = slot_param.shape[1]
    F = weight_in.shape[2]
    T = 2 * XY
    NZ = ZL * ZH
    rows = NZ * T
    PAIR = 2 * (D // LANES)
    DMA = pltpu.SemaphoreType.DMA
    anywhere = pl.BlockSpec(memory_space=pl.ANY)
    vmem = pltpu.VMEM
    scratch = [
        vmem((patches, D), BF16), vmem((D, S), BF16), vmem((patches, D), BF16),
        vmem((2, D, F), BF16), vmem((2, F, D), BF16),
        vmem((patches, S), F32), vmem((patches, S), F32), vmem((patches, S), BF16), vmem((patches, S), BF16),
        vmem((T * ZH * PAIR, LANES), F32),
        vmem((T, ZH * PAIR, LANES), BF16), vmem((T, ZH * PAIR, LANES), BF16),
        vmem((ZH, 2, T, D), BF16), vmem((NZ, 2, T, D), BF16),
        vmem((rows, F), F32), vmem((rows, F), F32), vmem((2, rows, F), BF16), vmem((2, rows, F), BF16),
        vmem((NZ, 2, T, D), BF16), vmem((NZ, 2, T, D), BF16),
        vmem((T, ZH * PAIR, LANES), BF16), vmem((T, ZH * PAIR, LANES), BF16),
        vmem((2, S, D), BF16),
        vmem((patches, D), BF16), vmem((2, D, F), BF16), vmem((2, F, D), BF16),
        vmem((T, 2, 8, LANES), F32), vmem((T, 2, 8, LANES), F32),
        vmem((2, 8, LANES), F32), vmem((NZ, 2, 8, LANES), F32),
        vmem((2, 8, LANES), F32), vmem((T, 2, 8, LANES), F32), vmem((S, D), F32),
        DMA((5,)), DMA((4,)), DMA((2,)), DMA((2,)), DMA((2,)), DMA((2,)),
        DMA, DMA, DMA((NZ,)), DMA((NZ,)), DMA((NZ,)), DMA((NZ,)), DMA, DMA,
        DMA, DMA, DMA, DMA, DMA, DMA,
    ]
    grad_tokens, grad_param, grad_win, grad_wout = pl.pallas_call(
        functools.partial(kernel, ZL, XY),
        out_shape=(
            jax.ShapeDtypeStruct((patches, D), BF16),
            jax.ShapeDtypeStruct((S, D), F32),
            jax.ShapeDtypeStruct(weight_in.shape, BF16),
            jax.ShapeDtypeStruct(weight_out.shape, BF16),
        ),
        in_specs=[anywhere] * 5,
        out_specs=[anywhere] * 4,
        scratch_shapes=scratch,
        compiler_params=pltpu.CompilerParams(
            collective_id=0, has_side_effects=True, vmem_limit_bytes=48 * 1024 * 1024
        ),
    )(tokens[0], slot_param, weight_in, weight_out, grad_out[0])
    return grad_tokens[None], grad_param.T, grad_win, grad_wout


def solution(mesh):
    ZL = mesh.shape["ex"] // 2
    XY = mesh.shape["ey"] // ZH
    split = Mesh(mesh.devices.reshape(ZL, 2, ZH, XY), AXES)
    return jax.shard_map(
        functools.partial(per_device, ZL, XY),
        mesh=split,
        in_specs=(P(ALL, None, None), P(), P(EY, None, EX), P(EY, EX, None), P(ALL, None, None)),
        out_specs=(P(ALL, None, None), P(), P(EY, None, EX), P(EY, EX, None)),
        check_vma=False,
    )
```

```python
import functools

import jax
import jax.numpy as jnp
from jax import lax
from jax.experimental import pallas as pl
from jax.experimental.pallas import tpu as pltpu
from jax.sharding import Mesh
from jax.sharding import PartitionSpec as P

AXES = ("zl", "core", "zh", "xy")
EX = ("zl", "core")
EY = ("zh", "xy")
ALL = AXES
ZH = 2
LANES = 128
F32 = jnp.float32
BF16 = jnp.bfloat16


def dot(a, b, ca, cb):
    return lax.dot_general(a, b, (((ca,), (cb,)), ((), ())), preferred_element_type=F32)


def softmax_along(values, axis):
    top = jnp.max(values, axis=axis, keepdims=True)
    expo = jnp.exp(values - top)
    return expo / jnp.sum(expo, axis=axis, keepdims=True)


def gelu_parts(pre):
    cdf = 0.5 * (1.0 + lax.erf(pre * 0.7071067811865476))
    slope = cdf + pre * jnp.exp(-0.5 * pre * pre) * 0.3989422804014327
    return (pre * cdf, slope)


def kernel(
    ZL, XY,
    tok_hbm, par_hbm, wi_hbm, wo_hbm, go_hbm,
    gt_out, gp_out, gwi_out, gwo_out,
    tok, par, go, wi, wo,
    disp, comb, disp_b, comb_b,
    rows32, send1, recv1, planes, gathered,
    pre_s, slope_s, hid, dpre,
    ysend, yin, send2, recv2, slots,
    gwi_v, gwo_v,
    xsend, xrecv, zsend, zrecv, usend, urecv,
    in_sem, out_sem, w_send, w_recv, g_send, g_recv,
    a_send, a_recv, b_send, b_recv, y_send, y_recv, c_send, c_recv,
    x_send, x_recv, z_send, z_recv, u_send, u_recv,
):
    T = 2 * XY
    NZ = ZL * ZH
    S, D = par.shape
    J = D // LANES
    PAIR = 2 * J
    zl = lax.axis_index("zl")
    core = lax.axis_index("core")
    zh = lax.axis_index("zh")
    xy = lax.axis_index("xy")
    me_t = xy * 2 + core
    me_z = zh * ZL + zl

    def in_plane(d):
        t = lax.rem(me_t + d, T)
        return t, (zl, lax.rem(t, 2), zh, lax.div(t, 2))

    def along_z(d):
        z = lax.rem(me_z + d, NZ)
        return z, (lax.rem(z, ZL), core, lax.div(z, ZL), xy)

    sibling = (zl, 1 - core, zh, xy)

    def remote(src, dst, send_sem, recv_sem, device):
        return pltpu.make_async_remote_copy(
            src_ref=src, dst_ref=dst, send_sem=send_sem, recv_sem=recv_sem,
            device_id=device, device_id_type=pl.DeviceIdType.MESH,
        )

    barrier = pltpu.get_barrier_semaphore()

    def greet_plane(d, carry):
        pl.semaphore_signal(barrier, inc=1, device_id=in_plane(d)[1], device_id_type=pl.DeviceIdType.MESH)
        return carry

    def greet_z(d, carry):
        pl.semaphore_signal(barrier, inc=1, device_id=along_z(d)[1], device_id_type=pl.DeviceIdType.MESH)
        return carry

    loads = [
        pltpu.make_async_copy(tok_hbm, tok, in_sem.at[0]),
        pltpu.make_async_copy(par_hbm, par, in_sem.at[1]),
        pltpu.make_async_copy(go_hbm, go, in_sem.at[2]),
        pltpu.make_async_copy(wi_hbm.at[core], wi.at[core], in_sem.at[3]),
        pltpu.make_async_copy(wo_hbm.at[core], wo.at[core], in_sem.at[4]),
    ]
    for load in loads:
        load.start()
    lax.fori_loop(1, T, greet_plane, 0)
    lax.fori_loop(1, NZ, greet_z, 0)

    def pack(part, h, w):
        for j in range(J):
            rows32[pl.ds(h * PAIR + w * J + j, T, stride=ZH * PAIR), :] = part[:, j * LANES : (j + 1) * LANES]

    def unpack(h, w, j):
        return rows32[pl.ds(h * PAIR + w * J + j, T, stride=ZH * PAIR), :].astype(BF16)

    def all_to_all(send, recv, send_sem, recv_sem):
        def go_to(d, carry):
            t, device = in_plane(d)
            remote(send.at[t], recv.at[me_t], send_sem, recv_sem, device).start()
            return carry

        lax.fori_loop(1, T, go_to, 0)

    def wait_for(ref, sem):
        pltpu.make_async_copy(ref, ref, sem).wait()

    def wait_all(ref, count, sem):
        wait_for(ref.at[pl.ds(0, count)], sem)

    loads[0].wait()
    loads[1].wait()
    logits = dot(tok[...], par[...], 1, 1)
    dispatch = softmax_along(logits, 0)
    combine = softmax_along(logits, 1)
    disp[...] = dispatch
    comb[...] = combine
    disp_b[...] = dispatch.astype(BF16)
    comb_b[...] = combine.astype(BF16)
    slot_in = dot(disp_b[...], tok[...], 0, 0)
    for h in range(ZH):
        pack(slot_in[h * T : (h + 1) * T], h, 0)
    loads[2].wait()
    slot_cot = dot(comb_b[...], go[...], 0, 0)
    for h in range(ZH):
        pack(slot_cot[h * T : (h + 1) * T], h, 1)
    send1[...] = rows32[...].astype(BF16).reshape(send1.shape)

    pl.semaphore_wait(barrier, T - 1 + NZ - 1)
    all_to_all(send1, recv1, a_send, a_recv)
    swap = [
        remote(wi_hbm.at[1 - core], wi.at[core], w_send.at[0], w_recv.at[0], sibling),
        remote(wo_hbm.at[1 - core], wo.at[core], w_send.at[1], w_recv.at[1], sibling),
    ]
    for copy in swap:
        copy.start()
    wait_all(send1, T - 1, a_send)
    wait_all(recv1, T - 1, a_recv)
    recv1[me_t] = send1[me_t]
    rows32[...] = recv1[...].reshape(rows32.shape).astype(F32)
    for h in range(ZH):
        for w in range(2):
            for j in range(J):
                planes[h, w, :, j * LANES : (j + 1) * LANES] = unpack(h, w, j)
    for w in range(2):
        gathered[w, me_z] = planes[zh, w]

    def send_planes(w):
        def one(d, carry):
            z, device = along_z(d)
            remote(planes.at[lax.div(z, ZL), w], gathered.at[w, me_z], b_send.at[w], b_recv.at[w], device).start()
            return carry

        lax.fori_loop(1, NZ, one, 0)

    def send_back(w):
        def one(d, carry):
            z, device = along_z(d)
            remote(ysend.at[w, z], yin.at[w, me_z], y_send.at[w], y_recv.at[w], device).start()
            return carry

        lax.fori_loop(1, NZ, one, 0)
        yin[w, me_z] = ysend[w, me_z]

    send_planes(0)
    send_planes(1)
    for copy in loads[3:] + swap:
        copy.wait()

    rows = NZ * T
    step = min(16, rows)

    def by_rows(body):
        def one(k, carry):
            body(pl.ds(pl.multiple_of(k * step, step), step))
            return carry

        lax.fori_loop(0, rows // step, one, 0)

    def whole(w):
        return gathered[w].reshape(rows, D)

    def pre_part(f):
        pre_s[...] = dot(whole(0), wi[f], 1, 0)

        def body(part):
            value, slope = gelu_parts(pre_s[part, :])
            hid[f, part, :] = value.astype(BF16)
            slope_s[f, part, :] = slope

        by_rows(body)

    def back_part(f):
        pre_s[...] = dot(whole(1), wo[f], 1, 1)

        def body(part):
            dpre[f, part, :] = (pre_s[part, :] * slope_s[f, part, :]).astype(BF16)

        by_rows(body)

    def out_part(w):
        if w == 0:
            total = dot(hid[0], wo[0], 1, 0) + dot(hid[1], wo[1], 1, 0)
        else:
            total = dot(dpre[0], wi[0], 1, 1) + dot(dpre[1], wi[1], 1, 1)
        ysend[w] = total.astype(BF16).reshape(ysend.shape[1:])

    def win_part(f):
        gwi_v[f] = dot(whole(0), dpre[f], 0, 0).astype(BF16)

    def wout_part(f):
        gwo_v[f] = dot(hid[f], whole(1), 0, 0).astype(BF16)

    wait_all(gathered.at[0], NZ - 1, b_recv.at[0])
    pre_part(0)
    pre_part(1)
    out_part(0)
    send_back(0)
    wait_all(gathered.at[1], NZ - 1, b_recv.at[1])
    back_part(0)
    back_part(1)
    out_part(1)
    send_back(1)
    for f in range(2):
        wout_part(f)
        win_part(f)
    stores = [
        pltpu.make_async_copy(gwi_v.at[core], gwi_out.at[core], out_sem.at[0]),
        pltpu.make_async_copy(gwo_v.at[core], gwo_out.at[core], out_sem.at[1]),
        remote(gwi_v.at[1 - core], gwi_out.at[core], g_send.at[0], g_recv.at[0], sibling),
        remote(gwo_v.at[1 - core], gwo_out.at[core], g_send.at[1], g_recv.at[1], sibling),
    ]
    for copy in stores:
        copy.start()
    for w in range(2):
        wait_all(gathered.at[w], NZ - 1, b_send.at[w])
        wait_all(ysend.at[w], NZ - 1, y_send.at[w])

    for w in range(2):
        wait_all(yin.at[w], NZ - 1, y_recv.at[w])
        for h in range(ZH):
            pack(jnp.sum(yin[w, h * ZL : (h + 1) * ZL].astype(F32), axis=0), h, w)
    send2[...] = rows32[...].astype(BF16).reshape(send2.shape)
    all_to_all(send2, recv2, c_send, c_recv)
    wait_all(send2, T - 1, c_send)
    wait_all(recv2, T - 1, c_recv)
    recv2[me_t] = send2[me_t]
    rows32[...] = recv2[...].reshape(rows32.shape).astype(F32)
    for h in range(ZH):
        for w in range(2):
            for j in range(J):
                slots[w, h * T : (h + 1) * T, j * LANES : (j + 1) * LANES] = unpack(h, w, j)

    d_combine = dot(go[...], slots[0], 1, 1)
    d_dispatch = dot(tok[...], slots[1], 1, 1)
    dispatch = disp[...]
    combine = comb[...]
    d_logits = dispatch * (d_dispatch - jnp.sum(dispatch * d_dispatch, axis=0, keepdims=True))
    d_logits = d_logits + combine * (d_combine - jnp.sum(combine * d_combine, axis=1, keepdims=True))
    logit_grad = d_logits.astype(BF16)
    local_param = dot(logit_grad, tok[...], 0, 0)

    R = min(16, S)
    tiles = [
        (k * R // 16, slice(k * R % 16, k * R % 16 + R), slice(r, r + R), slice(j * LANES, (j + 1) * LANES))
        for k, (r, j) in enumerate((r, j) for r in range(0, S, R) for j in range(J))
    ]
    for k, inside, row, column in tiles:
        xsend[k, inside, :] = local_param[row, column].astype(BF16)
    all_to_all(xsend, xrecv, x_send, x_recv)
    gt_out[...] = (dot(disp_b[...], slots[1], 1, 0) + dot(logit_grad, par[...], 1, 0)).astype(BF16)
    wait_all(xsend, T - 1, x_send)
    wait_all(xrecv, T - 1, x_recv)
    xrecv[me_t] = xsend[me_t]
    zsend[...] = jnp.sum(xrecv[...].astype(F32), axis=0)

    def send_sum(d, carry):
        remote(zsend, zrecv.at[me_z], z_send, z_recv, along_z(d)[1]).start()
        return carry

    lax.fori_loop(1, NZ, send_sum, 0)
    wait_all(zrecv, NZ - 1, z_send)
    wait_all(zrecv, NZ - 1, z_recv)
    zrecv[me_z] = zsend[...]
    usend[...] = jnp.sum(zrecv[...], axis=0).astype(BF16)

    def send_total(d, carry):
        remote(usend, urecv.at[me_t], u_send, u_recv, in_plane(d)[1]).start()
        return carry

    lax.fori_loop(1, T, send_total, 0)
    wait_all(urecv, T - 1, u_send)
    wait_all(urecv, T - 1, u_recv)
    urecv[me_t] = usend[...]
    for k, inside, row, column in tiles:
        gp_out[row, column] = urecv[k, inside, :].astype(F32)
    for copy in stores:
        copy.wait()


def deliver(gt, gp, gwi, gwo, gt_out, gp_out, gwi_out, gwo_out, gt_v, gp_v, gwi_v, gwo_v, in_sem, out_sem):
    parts = []
    for src, held, dst in ((gwi, gwi_v, gwi_out), (gwo, gwo_v, gwo_out)):
        half = src.shape[1] // 2
        for e in range(2):
            for low in (0, half):
                at = (e, pl.ds(low, half))
                parts.append((src.at[at], held.at[at], dst.at[at]))
    parts += [(gt, gt_v, gt_out), (gp, gp_v, gp_out)]
    ins = [pltpu.make_async_copy(src, held, in_sem.at[k]) for k, (src, held, _) in enumerate(parts)]
    outs = [pltpu.make_async_copy(held, dst, out_sem.at[k]) for k, (_, held, dst) in enumerate(parts)]
    for copy in ins:
        copy.start()
    for came, goes in zip(ins, outs):
        came.wait()
        goes.start()
    for copy in outs:
        copy.wait()


def per_device(ZL, XY, tokens, slot_param, weight_in, weight_out, grad_out):
    _, patches, D = tokens.shape
    S = slot_param.shape[1]
    F = weight_in.shape[2]
    T = 2 * XY
    NZ = ZL * ZH
    rows = NZ * T
    PAIR = 2 * (D // LANES)
    DMA = pltpu.SemaphoreType.DMA
    vmem = pltpu.VMEM
    anywhere = pl.BlockSpec(memory_space=pl.ANY)
    in_hbm = pl.BlockSpec(memory_space=pltpu.HBM)
    in_vmem = pl.BlockSpec(memory_space=pltpu.VMEM)
    scratch = [
        vmem((patches, D), BF16), vmem((S, D), BF16), vmem((patches, D), BF16),
        vmem((2, D, F), BF16), vmem((2, F, D), BF16),
        vmem((patches, S), F32), vmem((patches, S), F32), vmem((patches, S), BF16), vmem((patches, S), BF16),
        vmem((T * ZH * PAIR, LANES), F32),
        vmem((T, ZH * PAIR, LANES), BF16), vmem((T, ZH * PAIR, LANES), BF16),
        vmem((ZH, 2, T, D), BF16), vmem((2, NZ, T, D), BF16),
        vmem((rows, F), F32), vmem((2, rows, F), F32), vmem((2, rows, F), BF16), vmem((2, rows, F), BF16),
        vmem((2, NZ, T, D), BF16), vmem((2, NZ, T, D), BF16),
        vmem((T, ZH * PAIR, LANES), BF16), vmem((T, ZH * PAIR, LANES), BF16),
        vmem((2, S, D), BF16),
        vmem((2, D, F), BF16), vmem((2, F, D), BF16),
        vmem((T, 16, LANES), BF16), vmem((T, 16, LANES), BF16),
        vmem((16, LANES), F32), vmem((NZ, 16, LANES), F32),
        vmem((16, LANES), BF16), vmem((T, 16, LANES), BF16),
        DMA((5,)), DMA((2,)), DMA((2,)), DMA((2,)), DMA((2,)), DMA((2,)),
        DMA, DMA, DMA((2,)), DMA((2,)), DMA((2,)), DMA((2,)), DMA, DMA,
        DMA, DMA, DMA, DMA, DMA, DMA,
    ]
    shapes = (
        jax.ShapeDtypeStruct((patches, D), BF16),
        jax.ShapeDtypeStruct((S, D), F32),
        jax.ShapeDtypeStruct(weight_in.shape, BF16),
        jax.ShapeDtypeStruct(weight_out.shape, BF16),
    )
    results = pl.pallas_call(
        functools.partial(kernel, ZL, XY),
        out_shape=shapes,
        in_specs=[in_hbm] * 5,
        out_specs=[in_vmem, in_vmem, anywhere, anywhere],
        scratch_shapes=scratch,
        compiler_params=pltpu.CompilerParams(
            collective_id=0, has_side_effects=True, vmem_limit_bytes=60 * 1024 * 1024
        ),
    )(tokens[0], slot_param.T, weight_in, weight_out, grad_out[0])
    grad_tokens, grad_param, grad_win, grad_wout = pl.pallas_call(
        deliver,
        out_shape=shapes,
        in_specs=[anywhere] * 4,
        out_specs=[in_hbm] * 4,
        scratch_shapes=[vmem(shape.shape, shape.dtype) for shape in shapes] + [DMA((10,)), DMA((10,))],
        compiler_params=pltpu.CompilerParams(vmem_limit_bytes=60 * 1024 * 1024),
    )(*results)
    return grad_tokens[None], grad_param.T, grad_win, grad_wout


def solution(mesh):
    ZL = mesh.shape["ex"] // 2
    XY = mesh.shape["ey"] // ZH
    split = Mesh(mesh.devices.reshape(ZL, 2, ZH, XY), AXES)
    return jax.shard_map(
        functools.partial(per_device, ZL, XY),
        mesh=split,
        in_specs=(P(ALL, None, None), P(), P(EY, None, EX), P(EY, EX, None), P(ALL, None, None)),
        out_specs=(P(ALL, None, None), P(), P(EY, None, EX), P(EY, EX, None)),
        check_vma=False,
    )
```

```python
import functools

import jax
import jax.numpy as jnp
from jax import lax
from jax.experimental import pallas as pl
from jax.experimental.pallas import tpu as pltpu
from jax.sharding import Mesh
from jax.sharding import PartitionSpec as P

AXES = ("zl", "core", "zh", "xy")
EX = ("zl", "core")
EY = ("zh", "xy")
ALL = AXES
ZH = 2
LANES = 128
F32 = jnp.float32
BF16 = jnp.bfloat16


def dot(a, b, ca, cb):
    return lax.dot_general(a, b, (((ca,), (cb,)), ((), ())), preferred_element_type=F32)


def softmax_along(values, axis):
    top = jnp.max(values, axis=axis, keepdims=True)
    expo = jnp.exp(values - top)
    return expo / jnp.sum(expo, axis=axis, keepdims=True)


def gelu_parts(pre):
    cdf = 0.5 * (1.0 + lax.erf(pre * 0.7071067811865476))
    slope = cdf + pre * jnp.exp(-0.5 * pre * pre) * 0.3989422804014327
    return (pre * cdf, slope)


def kernel(
    ZL, XY,
    tok_hbm, par_hbm, wi_hbm, wo_hbm, go_hbm,
    gt_out, gp_out, gwi_out, gwo_out,
    tok, par, go, wi, wo,
    disp, comb, disp_b, comb_b,
    rows32, send1, recv1, planes, gathered,
    pre_s, slope_s, hid, dpre,
    ysend, yin, ypair, fin, send2, recv2, slots,
    gwi_v, gwo_v,
    xsend, xrecv, zsend, zrecv, usend, urecv,
    in_sem, out_sem, w_send, w_recv, g_send, g_recv,
    a_send, a_recv, b_send, b_recv, y_send, y_recv, c_send, c_recv,
    x_send, x_recv, z_send, z_recv, u_send, u_recv,
):
    T = 2 * XY
    NZ = ZL * ZH
    S, D = par.shape
    J = D // LANES
    zl = lax.axis_index("zl")
    core = lax.axis_index("core")
    zh = lax.axis_index("zh")
    xy = lax.axis_index("xy")
    me_t = xy * 2 + core
    me_z = zh * ZL + zl

    def in_plane(d):
        t = lax.rem(me_t + d, T)
        return t, (zl, lax.rem(t, 2), zh, lax.div(t, 2))

    def along_z(d):
        z = lax.rem(me_z + d, NZ)
        return z, (lax.rem(z, ZL), core, lax.div(z, ZL), xy)

    sibling = (zl, 1 - core, zh, xy)

    def remote(src, dst, send_sem, recv_sem, device):
        return pltpu.make_async_remote_copy(
            src_ref=src, dst_ref=dst, send_sem=send_sem, recv_sem=recv_sem,
            device_id=device, device_id_type=pl.DeviceIdType.MESH,
        )

    barrier = pltpu.get_barrier_semaphore()

    def greet_plane(d, carry):
        pl.semaphore_signal(barrier, inc=1, device_id=in_plane(d)[1], device_id_type=pl.DeviceIdType.MESH)
        return carry

    def greet_z(d, carry):
        pl.semaphore_signal(barrier, inc=1, device_id=along_z(d)[1], device_id_type=pl.DeviceIdType.MESH)
        return carry

    loads = [
        pltpu.make_async_copy(tok_hbm, tok, in_sem.at[0]),
        pltpu.make_async_copy(par_hbm, par, in_sem.at[1]),
        pltpu.make_async_copy(go_hbm, go, in_sem.at[2]),
        pltpu.make_async_copy(wi_hbm.at[core], wi.at[core], in_sem.at[3]),
        pltpu.make_async_copy(wo_hbm.at[core], wo.at[core], in_sem.at[4]),
    ]
    for load in loads:
        load.start()
    lax.fori_loop(1, T, greet_plane, 0)
    lax.fori_loop(1, NZ, greet_z, 0)

    def pack(part, h, w):
        for j in range(J):
            rows32[w, pl.ds(h * J + j, T, stride=ZH * J), :] = part[:, j * LANES : (j + 1) * LANES]

    def messages(w):
        return rows32[w].reshape(T, ZH * J, LANES).astype(BF16)

    def unpack(h, w, j):
        return rows32[w, pl.ds(h * J + j, T, stride=ZH * J), :].astype(BF16)

    def arrived(send, recv, w):
        recv[w, me_t] = send[w, me_t]
        rows32[w] = recv[w].reshape(T * ZH * J, LANES).astype(F32)

    def all_to_all(send, recv, send_sem, recv_sem):
        def go_to(d, carry):
            t, device = in_plane(d)
            remote(send.at[t], recv.at[me_t], send_sem, recv_sem, device).start()
            return carry

        lax.fori_loop(1, T, go_to, 0)

    def wait_for(ref, sem):
        pltpu.make_async_copy(ref, ref, sem).wait()

    def wait_all(ref, count, sem):
        wait_for(ref.at[pl.ds(0, count)], sem)

    loads[0].wait()
    loads[1].wait()
    logits = dot(tok[...], par[...], 1, 1)
    dispatch = softmax_along(logits, 0)
    disp[...] = dispatch
    disp_b[...] = dispatch.astype(BF16)
    slot_in = dot(disp_b[...], tok[...], 0, 0)
    for h in range(ZH):
        pack(slot_in[h * T : (h + 1) * T], h, 0)
    send1[0] = messages(0)
    pl.semaphore_wait(barrier, T - 1 + NZ - 1)
    all_to_all(send1.at[0], recv1.at[0], a_send.at[0], a_recv.at[0])
    combine = softmax_along(logits, 1)
    comb[...] = combine
    comb_b[...] = combine.astype(BF16)
    loads[2].wait()
    slot_cot = dot(comb_b[...], go[...], 0, 0)
    for h in range(ZH):
        pack(slot_cot[h * T : (h + 1) * T], h, 1)
    send1[1] = messages(1)
    all_to_all(send1.at[1], recv1.at[1], a_send.at[1], a_recv.at[1])
    swap = [
        remote(wi_hbm.at[1 - core], wi.at[core], w_send.at[0], w_recv.at[0], sibling),
        remote(wo_hbm.at[1 - core], wo.at[core], w_send.at[1], w_recv.at[1], sibling),
    ]
    for copy in swap:
        copy.start()

    odd = lax.rem(zl, 2)
    partner = (zl + 1 - 2 * odd, core, zh, xy)
    mine = (1 - zh) * ZL + 2 * (1 - odd)
    theirs = (1 - zh) * ZL + 2 * odd

    def in_group(d):
        k = lax.rem(zl + d, ZL)
        return zh * ZL + k, (k, core, zh, xy)

    def send_planes(w):
        wait_all(send1.at[w], T - 1, a_send.at[w])
        wait_all(recv1.at[w], T - 1, a_recv.at[w])
        arrived(send1, recv1, w)
        for h in range(ZH):
            for j in range(J):
                planes[h, w, :, j * LANES : (j + 1) * LANES] = unpack(h, w, j)
        first = 1 - lax.div(zl, 2)
        for k in range(2):
            device = (first + 2 * k, core, 1 - zh, xy)
            remote(planes.at[1 - zh, w], gathered.at[w, me_z], b_send.at[w, 0], b_recv.at[w, 1], device).start()
        for d in (2, 1, 3):
            remote(planes.at[zh, w], gathered.at[w, me_z], b_send.at[w, 0], b_recv.at[w, 0], in_group(d)[1]).start()
        gathered[w, me_z] = planes[zh, w]

    def pass_on(w):
        block = gathered.at[w, pl.ds(mine, 2)]
        wait_for(block, b_recv.at[w, 1])
        remote(block, block, b_send.at[w, 1], b_recv.at[w, 2], partner).start()

    def all_here(w):
        wait_for(gathered.at[w, pl.ds(zh * ZL, ZL - 1)], b_recv.at[w, 0])
        wait_for(gathered.at[w, pl.ds(theirs, 2)], b_recv.at[w, 2])

    def send_back(w):
        remote(ysend.at[w, pl.ds(theirs, 2)], ypair.at[w], y_send.at[w, 1], y_recv.at[w, 1], partner).start()
        for d in (2, 1, 3):
            z, device = in_group(d)
            remote(ysend.at[w, z], yin.at[w, zl], y_send.at[w, 0], y_recv.at[w, 0], device).start()
        yin[w, zl] = ysend[w, me_z]

    def send_pairs(w):
        wait_for(ypair.at[w], y_recv.at[w, 1])
        for k in range(2):
            ysend[w, mine + k] = (ysend[w, mine + k].astype(F32) + ypair[w, k].astype(F32)).astype(BF16)
            device = (2 * (1 - odd) + k, core, 1 - zh, xy)
            remote(ysend.at[w, mine + k], yin.at[w, ZL + lax.div(zl, 2)], y_send.at[w, 2], y_recv.at[w, 2], device).start()

    def sums_back(w):
        wait_for(yin.at[w, pl.ds(0, ZL - 1)], y_recv.at[w, 0])
        wait_for(yin.at[w, pl.ds(ZL, 2)], y_recv.at[w, 2])
        fin[zh] = jnp.sum(yin[w, :ZL].astype(F32), axis=0)
        fin[1 - zh] = yin[w, ZL].astype(F32) + yin[w, ZL + 1].astype(F32)
        for h in range(ZH):
            pack(fin[h], h, w)
        send2[w] = messages(w)
        all_to_all(send2.at[w], recv2.at[w], c_send.at[w], c_recv.at[w])

    def take_slots(w):
        wait_all(recv2.at[w], T - 1, c_recv.at[w])
        arrived(send2, recv2, w)
        for h in range(ZH):
            for j in range(J):
                slots[w, h * T : (h + 1) * T, j * LANES : (j + 1) * LANES] = unpack(h, w, j)

    send_planes(0)
    send_planes(1)
    for copy in loads[3:] + swap:
        copy.wait()
    pass_on(0)

    rows = NZ * T
    step = min(16, rows)

    def by_rows(body):
        def one(k, carry):
            body(pl.ds(pl.multiple_of(k * step, step), step))
            return carry

        lax.fori_loop(0, rows // step, one, 0)

    def whole(w):
        return gathered[w].reshape(rows, D)

    def pre_part(f):
        pre_s[...] = dot(whole(0), wi[f], 1, 0)

        def body(part):
            value, slope = gelu_parts(pre_s[part, :])
            hid[f, part, :] = value.astype(BF16)
            slope_s[f, part, :] = slope

        by_rows(body)

    def back_part(f):
        pre_s[...] = dot(whole(1), wo[f], 1, 1)

        def body(part):
            dpre[f, part, :] = (pre_s[part, :] * slope_s[f, part, :]).astype(BF16)

        by_rows(body)

    def out_part(w):
        if w == 0:
            total = dot(hid[0], wo[0], 1, 0) + dot(hid[1], wo[1], 1, 0)
        else:
            total = dot(dpre[0], wi[0], 1, 1) + dot(dpre[1], wi[1], 1, 1)
        ysend[w] = total.astype(BF16).reshape(ysend.shape[1:])

    def win_part(f):
        gwi_v[f] = dot(whole(0), dpre[f], 0, 0).astype(BF16)

    def wout_part(f):
        gwo_v[f] = dot(hid[f], whole(1), 0, 0).astype(BF16)

    all_here(0)
    pre_part(0)
    pass_on(1)
    pre_part(1)
    out_part(0)
    send_back(0)
    all_here(1)
    back_part(0)
    send_pairs(0)
    back_part(1)
    out_part(1)
    send_back(1)
    for f in range(2):
        wout_part(f)
    send_pairs(1)
    for f in range(2):
        win_part(f)
    stores = [
        pltpu.make_async_copy(gwi_v.at[core], gwi_out.at[core], out_sem.at[0]),
        pltpu.make_async_copy(gwo_v.at[core], gwo_out.at[core], out_sem.at[1]),
        remote(gwi_v.at[1 - core], gwi_out.at[core], g_send.at[0], g_recv.at[0], sibling),
        remote(gwo_v.at[1 - core], gwo_out.at[core], g_send.at[1], g_recv.at[1], sibling),
    ]
    for copy in stores:
        copy.start()

    sums_back(0)
    take_slots(0)
    d_combine = dot(go[...], slots[0], 1, 1)
    combine = comb[...]
    by_combine = combine * (d_combine - jnp.sum(combine * d_combine, axis=1, keepdims=True))
    sums_back(1)
    for w in range(2):
        wait_all(gathered.at[w], ZL - 1 + 2, b_send.at[w, 0])
        wait_all(gathered.at[w], 2, b_send.at[w, 1])
        wait_all(ysend.at[w], ZL - 1, y_send.at[w, 0])
        wait_all(ysend.at[w], 2, y_send.at[w, 1])
        wait_all(ysend.at[w], 2, y_send.at[w, 2])
        wait_all(send2.at[w], T - 1, c_send.at[w])
    take_slots(1)
    d_dispatch = dot(tok[...], slots[1], 1, 1)
    dispatch = disp[...]
    d_logits = dispatch * (d_dispatch - jnp.sum(dispatch * d_dispatch, axis=0, keepdims=True))
    d_logits = d_logits + by_combine
    logit_grad = d_logits.astype(BF16)
    local_param = dot(logit_grad, tok[...], 0, 0)

    R = min(16, S)
    tiles = [
        (k * R // 16, slice(k * R % 16, k * R % 16 + R), slice(r, r + R), slice(j * LANES, (j + 1) * LANES))
        for k, (r, j) in enumerate((r, j) for r in range(0, S, R) for j in range(J))
    ]
    for k, inside, row, column in tiles:
        xsend[k, inside, :] = local_param[row, column].astype(BF16)
    all_to_all(xsend, xrecv, x_send, x_recv)
    gt_out[...] = (dot(disp_b[...], slots[1], 1, 0) + dot(logit_grad, par[...], 1, 0)).astype(BF16)
    wait_all(xsend, T - 1, x_send)
    wait_all(xrecv, T - 1, x_recv)
    xrecv[me_t] = xsend[me_t]
    zsend[...] = jnp.sum(xrecv[...].astype(F32), axis=0).astype(BF16)

    def send_sum(d, carry):
        remote(zsend, zrecv.at[me_z], z_send, z_recv, along_z(d)[1]).start()
        return carry

    lax.fori_loop(1, NZ, send_sum, 0)
    wait_all(zrecv, NZ - 1, z_send)
    wait_all(zrecv, NZ - 1, z_recv)
    zrecv[me_z] = zsend[...]
    usend[...] = jnp.sum(zrecv[...].astype(F32), axis=0).astype(BF16)

    def send_total(d, carry):
        remote(usend, urecv.at[me_t], u_send, u_recv, in_plane(d)[1]).start()
        return carry

    lax.fori_loop(1, T, send_total, 0)
    wait_all(urecv, T - 1, u_send)
    wait_all(urecv, T - 1, u_recv)
    urecv[me_t] = usend[...]
    for k, inside, row, column in tiles:
        gp_out[row, column] = urecv[k, inside, :].astype(F32)
    for copy in stores:
        copy.wait()


def deliver(gt, gp, gwi, gwo, gt_out, gp_out, gwi_out, gwo_out, gt_v, gp_v, gwi_v, gwo_v, in_sem, out_sem):
    parts = []
    for src, held, dst in ((gwi, gwi_v, gwi_out), (gwo, gwo_v, gwo_out)):
        half = src.shape[1] // 2
        for e in range(2):
            for low in (0, half):
                at = (e, pl.ds(low, half))
                parts.append((src.at[at], held.at[at], dst.at[at]))
    parts += [(gt, gt_v, gt_out), (gp, gp_v, gp_out)]
    ins = [pltpu.make_async_copy(src, held, in_sem.at[k]) for k, (src, held, _) in enumerate(parts)]
    outs = [pltpu.make_async_copy(held, dst, out_sem.at[k]) for k, (_, held, dst) in enumerate(parts)]
    for copy in ins:
        copy.start()
    for came, goes in zip(ins, outs):
        came.wait()
        goes.start()
    for copy in outs:
        copy.wait()


def per_device(ZL, XY, tokens, slot_param, weight_in, weight_out, grad_out):
    _, patches, D = tokens.shape
    S = slot_param.shape[1]
    F = weight_in.shape[2]
    T = 2 * XY
    NZ = ZL * ZH
    rows = NZ * T
    PER = ZH * (D // LANES)
    DMA = pltpu.SemaphoreType.DMA
    vmem = pltpu.VMEM
    anywhere = pl.BlockSpec(memory_space=pl.ANY)
    in_hbm = pl.BlockSpec(memory_space=pltpu.HBM)
    in_vmem = pl.BlockSpec(memory_space=pltpu.VMEM)
    scratch = [
        vmem((patches, D), BF16), vmem((S, D), BF16), vmem((patches, D), BF16),
        vmem((2, D, F), BF16), vmem((2, F, D), BF16),
        vmem((patches, S), F32), vmem((patches, S), F32), vmem((patches, S), BF16), vmem((patches, S), BF16),
        vmem((2, T * PER, LANES), F32), vmem((2, T, PER, LANES), BF16), vmem((2, T, PER, LANES), BF16),
        vmem((ZH, 2, T, D), BF16), vmem((2, NZ, T, D), BF16),
        vmem((rows, F), F32), vmem((2, rows, F), F32), vmem((2, rows, F), BF16), vmem((2, rows, F), BF16),
        vmem((2, NZ, T, D), BF16), vmem((2, ZL + 2, T, D), BF16), vmem((2, 2, T, D), BF16), vmem((ZH, T, D), F32),
        vmem((2, T, PER, LANES), BF16), vmem((2, T, PER, LANES), BF16),
        vmem((2, S, D), BF16),
        vmem((2, D, F), BF16), vmem((2, F, D), BF16),
        vmem((T, 16, LANES), BF16), vmem((T, 16, LANES), BF16),
        vmem((16, LANES), BF16), vmem((NZ, 16, LANES), BF16),
        vmem((16, LANES), BF16), vmem((T, 16, LANES), BF16),
        DMA((5,)), DMA((2,)), DMA((2,)), DMA((2,)), DMA((2,)), DMA((2,)),
        DMA((2,)), DMA((2,)), DMA((2, 2)), DMA((2, 3)), DMA((2, 3)), DMA((2, 3)), DMA((2,)), DMA((2,)),
        DMA, DMA, DMA, DMA, DMA, DMA,
    ]
    shapes = (
        jax.ShapeDtypeStruct((patches, D), BF16),
        jax.ShapeDtypeStruct((S, D), F32),
        jax.ShapeDtypeStruct(weight_in.shape, BF16),
        jax.ShapeDtypeStruct(weight_out.shape, BF16),
    )
    results = pl.pallas_call(
        functools.partial(kernel, ZL, XY),
        out_shape=shapes,
        in_specs=[in_hbm] * 5,
        out_specs=[in_vmem, in_vmem, anywhere, anywhere],
        scratch_shapes=scratch,
        compiler_params=pltpu.CompilerParams(
            collective_id=0, has_side_effects=True, vmem_limit_bytes=60 * 1024 * 1024
        ),
    )(tokens[0], slot_param.T, weight_in, weight_out, grad_out[0])
    grad_tokens, grad_param, grad_win, grad_wout = pl.pallas_call(
        deliver,
        out_shape=shapes,
        in_specs=[anywhere] * 4,
        out_specs=[in_hbm] * 4,
        scratch_shapes=[vmem(shape.shape, shape.dtype) for shape in shapes] + [DMA((10,)), DMA((10,))],
        compiler_params=pltpu.CompilerParams(vmem_limit_bytes=60 * 1024 * 1024),
    )(*results)
    return grad_tokens[None], grad_param.T, grad_win, grad_wout


def solution(mesh):
    ZL = mesh.shape["ex"] // 2
    XY = mesh.shape["ey"] // ZH
    split = Mesh(mesh.devices.reshape(ZL, 2, ZH, XY), AXES)
    return jax.shard_map(
        functools.partial(per_device, ZL, XY),
        mesh=split,
        in_specs=(P(ALL, None, None), P(), P(EY, None, EX), P(EY, EX, None), P(ALL, None, None)),
        out_specs=(P(ALL, None, None), P(), P(EY, None, EX), P(EY, EX, None)),
        check_vma=False,
    )
```

```python
import functools

import jax
import jax.numpy as jnp
from jax import lax
from jax.experimental import pallas as pl
from jax.experimental.pallas import tpu as pltpu
from jax.sharding import Mesh
from jax.sharding import PartitionSpec as P

AXES = ("zl", "core", "zh", "xy")
EX = ("zl", "core")
EY = ("zh", "xy")
ALL = AXES
ZH = 2
LANES = 128
F32 = jnp.float32
BF16 = jnp.bfloat16


def dot(a, b, ca, cb):
    return lax.dot_general(a, b, (((ca,), (cb,)), ((), ())), preferred_element_type=F32)


def softmax_along(values, axis):
    top = jnp.max(values, axis=axis, keepdims=True)
    expo = jnp.exp(values - top)
    return expo / jnp.sum(expo, axis=axis, keepdims=True)


def gelu_parts(pre):
    cdf = 0.5 * (1.0 + lax.erf(pre * 0.7071067811865476))
    slope = cdf + pre * jnp.exp(-0.5 * pre * pre) * 0.3989422804014327
    return (pre * cdf, slope)


def kernel(
    ZL, XY,
    tok_hbm, par_hbm, wi_hbm, wo_hbm, go_hbm,
    gt_out, gp_out, gwi_out, gwo_out,
    tok, par, go, wi, wo,
    disp, comb, disp_b, comb_b,
    rows32, send1, recv1, planes, gathered,
    pre_s, slope_s, hid, dpre,
    ysend, yin, ypair, fin, send2, recv2, slots,
    gwi_v, gwo_v,
    xsend, xrecv, zsend, zrecv, usend, urecv,
    in_sem, out_sem, w_send, w_recv, g_send, g_recv,
    a_send, a_recv, b_send, b_recv, y_send, y_recv, c_send, c_recv,
    x_send, x_recv, z_send, z_recv, u_send, u_recv,
):
    T = 2 * XY
    NZ = ZL * ZH
    S, D = par.shape
    J = D // LANES
    zl = lax.axis_index("zl")
    core = lax.axis_index("core")
    zh = lax.axis_index("zh")
    xy = lax.axis_index("xy")
    me_t = xy * 2 + core
    me_z = zh * ZL + zl

    def in_plane(d):
        t = lax.rem(me_t + d, T)
        return t, (zl, lax.rem(t, 2), zh, lax.div(t, 2))

    def along_z(d):
        z = lax.rem(me_z + d, NZ)
        return z, (lax.rem(z, ZL), core, lax.div(z, ZL), xy)

    sibling = (zl, 1 - core, zh, xy)

    def remote(src, dst, send_sem, recv_sem, device):
        return pltpu.make_async_remote_copy(
            src_ref=src, dst_ref=dst, send_sem=send_sem, recv_sem=recv_sem,
            device_id=device, device_id_type=pl.DeviceIdType.MESH,
        )

    barrier = pltpu.get_barrier_semaphore()

    def greet_plane(d, carry):
        pl.semaphore_signal(barrier, inc=1, device_id=in_plane(d)[1], device_id_type=pl.DeviceIdType.MESH)
        return carry

    def greet_z(d, carry):
        pl.semaphore_signal(barrier, inc=1, device_id=along_z(d)[1], device_id_type=pl.DeviceIdType.MESH)
        return carry

    loads = [
        pltpu.make_async_copy(tok_hbm, tok, in_sem.at[0]),
        pltpu.make_async_copy(par_hbm, par, in_sem.at[1]),
        pltpu.make_async_copy(go_hbm, go, in_sem.at[2]),
        pltpu.make_async_copy(wi_hbm.at[core], wi.at[core], in_sem.at[3]),
        pltpu.make_async_copy(wo_hbm.at[core], wo.at[core], in_sem.at[4]),
    ]
    for load in loads:
        load.start()
    lax.fori_loop(1, T, greet_plane, 0)
    lax.fori_loop(1, NZ, greet_z, 0)

    def pack(part, h, w):
        for j in range(J):
            rows32[w, pl.ds(h * J + j, T, stride=ZH * J), :] = part[:, j * LANES : (j + 1) * LANES]

    def messages(w):
        return rows32[w].reshape(T, ZH * J, LANES).astype(BF16)

    def unpack(h, w, j):
        return rows32[w, pl.ds(h * J + j, T, stride=ZH * J), :].astype(BF16)

    def arrived(send, recv, w):
        recv[w, me_t] = send[w, me_t]
        rows32[w] = recv[w].reshape(T * ZH * J, LANES).astype(F32)

    def all_to_all(send, recv, send_sem, recv_sem):
        def go_to(d, carry):
            t, device = in_plane(d)
            remote(send.at[t], recv.at[me_t], send_sem, recv_sem, device).start()
            return carry

        lax.fori_loop(1, T, go_to, 0)

    def wait_for(ref, sem):
        pltpu.make_async_copy(ref, ref, sem).wait()

    def wait_all(ref, count, sem):
        wait_for(ref.at[pl.ds(0, count)], sem)

    loads[0].wait()
    loads[1].wait()
    logits = dot(tok[...], par[...], 1, 1)
    dispatch = softmax_along(logits, 0)
    disp[...] = dispatch
    disp_b[...] = dispatch.astype(BF16)
    slot_in = dot(disp_b[...], tok[...], 0, 0)
    for h in range(ZH):
        pack(slot_in[h * T : (h + 1) * T], h, 0)
    send1[0] = messages(0)
    pl.semaphore_wait(barrier, T - 1 + NZ - 1)
    all_to_all(send1.at[0], recv1.at[0], a_send.at[0], a_recv.at[0])
    combine = softmax_along(logits, 1)
    comb[...] = combine
    comb_b[...] = combine.astype(BF16)
    loads[2].wait()
    slot_cot = dot(comb_b[...], go[...], 0, 0)
    for h in range(ZH):
        pack(slot_cot[h * T : (h + 1) * T], h, 1)
    send1[1] = messages(1)
    all_to_all(send1.at[1], recv1.at[1], a_send.at[1], a_recv.at[1])
    swap = [
        remote(wi_hbm.at[1 - core], wi.at[core], w_send.at[0], w_recv.at[0], sibling),
        remote(wo_hbm.at[1 - core], wo.at[core], w_send.at[1], w_recv.at[1], sibling),
    ]
    for copy in swap:
        copy.start()

    odd = lax.rem(zl, 2)
    partner = (zl + 1 - 2 * odd, core, zh, xy)
    mine = (1 - zh) * ZL + 2 * (1 - odd)
    theirs = (1 - zh) * ZL + 2 * odd

    def in_group(d):
        k = lax.rem(zl + d, ZL)
        return zh * ZL + k, (k, core, zh, xy)

    def send_planes(w):
        wait_all(send1.at[w], T - 1, a_send.at[w])
        wait_all(recv1.at[w], T - 1, a_recv.at[w])
        arrived(send1, recv1, w)
        for h in range(ZH):
            for j in range(J):
                planes[h, w, :, j * LANES : (j + 1) * LANES] = unpack(h, w, j)
        first = 1 - lax.div(zl, 2)
        for k in range(2):
            device = (first + 2 * k, core, 1 - zh, xy)
            remote(planes.at[1 - zh, w], gathered.at[w, me_z], b_send.at[w, 0], b_recv.at[w, 1], device).start()
        for d in (2, 1, 3):
            remote(planes.at[zh, w], gathered.at[w, me_z], b_send.at[w, 0], b_recv.at[w, 0], in_group(d)[1]).start()
        gathered[w, me_z] = planes[zh, w]

    def pass_on(w):
        block = gathered.at[w, pl.ds(mine, 2)]
        wait_for(block, b_recv.at[w, 1])
        remote(block, block, b_send.at[w, 1], b_recv.at[w, 2], partner).start()

    def all_here(w):
        wait_for(gathered.at[w, pl.ds(zh * ZL, ZL - 1)], b_recv.at[w, 0])
        wait_for(gathered.at[w, pl.ds(theirs, 2)], b_recv.at[w, 2])

    def send_back(w):
        remote(ysend.at[w, pl.ds(theirs, 2)], ypair.at[w], y_send.at[w, 1], y_recv.at[w, 1], partner).start()
        for d in (2, 1, 3):
            z, device = in_group(d)
            remote(ysend.at[w, z], yin.at[w, zl], y_send.at[w, 0], y_recv.at[w, 0], device).start()
        yin[w, zl] = ysend[w, me_z]

    def send_pairs(w):
        wait_for(ypair.at[w], y_recv.at[w, 1])
        for k in range(2):
            ysend[w, mine + k] = (ysend[w, mine + k].astype(F32) + ypair[w, k].astype(F32)).astype(BF16)
            device = (2 * (1 - odd) + k, core, 1 - zh, xy)
            remote(ysend.at[w, mine + k], yin.at[w, ZL + lax.div(zl, 2)], y_send.at[w, 2], y_recv.at[w, 2], device).start()

    def sums_back(w):
        wait_for(yin.at[w, pl.ds(0, ZL - 1)], y_recv.at[w, 0])
        wait_for(yin.at[w, pl.ds(ZL, 2)], y_recv.at[w, 2])
        fin[zh] = jnp.sum(yin[w, :ZL].astype(F32), axis=0)
        fin[1 - zh] = yin[w, ZL].astype(F32) + yin[w, ZL + 1].astype(F32)
        for h in range(ZH):
            pack(fin[h], h, w)
        send2[w] = messages(w)
        all_to_all(send2.at[w], recv2.at[w], c_send.at[w], c_recv.at[w])

    def take_slots(w):
        wait_all(recv2.at[w], T - 1, c_recv.at[w])
        arrived(send2, recv2, w)
        for h in range(ZH):
            for j in range(J):
                slots[w, h * T : (h + 1) * T, j * LANES : (j + 1) * LANES] = unpack(h, w, j)

    send_planes(0)
    send_planes(1)
    for copy in loads[3:] + swap:
        copy.wait()
    pass_on(0)

    rows = NZ * T
    step = min(16, rows)

    def by_rows(body):
        def one(k, carry):
            body(pl.ds(pl.multiple_of(k * step, step), step))
            return carry

        lax.fori_loop(0, rows // step, one, 0)

    def whole(w):
        return gathered[w].reshape(rows, D)

    def pre_part(f):
        pre_s[...] = dot(whole(0), wi[f], 1, 0)

        def body(part):
            value, slope = gelu_parts(pre_s[part, :])
            hid[f, part, :] = value.astype(BF16)
            slope_s[f, part, :] = slope

        by_rows(body)

    def back_part(f):
        pre_s[...] = dot(whole(1), wo[f], 1, 1)

        def body(part):
            dpre[f, part, :] = (pre_s[part, :] * slope_s[f, part, :]).astype(BF16)

        by_rows(body)

    def out_part(w):
        if w == 0:
            total = dot(hid[0], wo[0], 1, 0) + dot(hid[1], wo[1], 1, 0)
        else:
            total = dot(dpre[0], wi[0], 1, 1) + dot(dpre[1], wi[1], 1, 1)
        ysend[w] = total.astype(BF16).reshape(ysend.shape[1:])

    def win_part(f):
        gwi_v[f] = dot(whole(0), dpre[f], 0, 0).astype(BF16)

    def wout_part(f):
        gwo_v[f] = dot(hid[f], whole(1), 0, 0).astype(BF16)

    all_here(0)
    pre_part(0)
    pass_on(1)
    pre_part(1)
    out_part(0)
    send_back(0)
    all_here(1)
    back_part(0)
    send_pairs(0)
    back_part(1)
    out_part(1)
    send_back(1)
    for f in range(2):
        wout_part(f)
    send_pairs(1)
    for f in range(2):
        win_part(f)
    stores = [
        pltpu.make_async_copy(gwi_v.at[core], gwi_out.at[core], out_sem.at[0]),
        pltpu.make_async_copy(gwo_v.at[core], gwo_out.at[core], out_sem.at[1]),
        remote(gwi_v.at[1 - core], gwi_out.at[core], g_send.at[0], g_recv.at[0], sibling),
        remote(gwo_v.at[1 - core], gwo_out.at[core], g_send.at[1], g_recv.at[1], sibling),
    ]
    for copy in stores:
        copy.start()

    sums_back(0)
    take_slots(0)
    d_combine = dot(go[...], slots[0], 1, 1)
    combine = comb[...]
    by_combine = combine * (d_combine - jnp.sum(combine * d_combine, axis=1, keepdims=True))
    sums_back(1)
    for w in range(2):
        wait_all(gathered.at[w], ZL - 1 + 2, b_send.at[w, 0])
        wait_all(gathered.at[w], 2, b_send.at[w, 1])
        wait_all(ysend.at[w], ZL - 1, y_send.at[w, 0])
        wait_all(ysend.at[w], 2, y_send.at[w, 1])
        wait_all(ysend.at[w], 2, y_send.at[w, 2])
        wait_all(send2.at[w], T - 1, c_send.at[w])
    take_slots(1)
    d_dispatch = dot(tok[...], slots[1], 1, 1)
    dispatch = disp[...]
    d_logits = dispatch * (d_dispatch - jnp.sum(dispatch * d_dispatch, axis=0, keepdims=True))
    d_logits = d_logits + by_combine
    logit_grad = d_logits.astype(BF16)
    local_param = dot(logit_grad, tok[...], 0, 0)

    R = min(16, S)
    tiles = [
        (k * R // 16, slice(k * R % 16, k * R % 16 + R), slice(r, r + R), slice(j * LANES, (j + 1) * LANES))
        for k, (r, j) in enumerate((r, j) for r in range(0, S, R) for j in range(J))
    ]
    for k, inside, row, column in tiles:
        xsend[k, inside, :] = local_param[row, column].astype(BF16)
    all_to_all(xsend, xrecv, x_send, x_recv)
    gt_out[...] = (dot(disp_b[...], slots[1], 1, 0) + dot(logit_grad, par[...], 1, 0)).astype(BF16)
    wait_all(xsend, T - 1, x_send)
    wait_all(xrecv, T - 1, x_recv)
    xrecv[me_t] = xsend[me_t]
    zsend[...] = jnp.sum(xrecv[...].astype(F32), axis=0).astype(BF16)

    def send_sum(d, carry):
        remote(zsend, zrecv.at[me_z], z_send, z_recv, along_z(d)[1]).start()
        return carry

    lax.fori_loop(1, NZ, send_sum, 0)
    wait_all(zrecv, NZ - 1, z_send)
    wait_all(zrecv, NZ - 1, z_recv)
    zrecv[me_z] = zsend[...]
    usend[...] = jnp.sum(zrecv[...].astype(F32), axis=0).astype(BF16)

    def send_total(d, carry):
        remote(usend, urecv.at[me_t], u_send, u_recv, in_plane(d)[1]).start()
        return carry

    lax.fori_loop(1, T, send_total, 0)
    wait_all(urecv, T - 1, u_send)
    wait_all(urecv, T - 1, u_recv)
    urecv[me_t] = usend[...]
    for k, inside, row, column in tiles:
        gp_out[row, column] = urecv[k, inside, :].astype(F32)
    for copy in stores:
        copy.wait()


def deliver(gt, gp, gwi, gwo, gt_out, gp_out, gwi_out, gwo_out, sem):
    pairs = ((gwi, gwi_out), (gwo, gwo_out), (gt, gt_out), (gp, gp_out))
    copies = [pltpu.make_async_copy(src, dst, sem.at[k]) for k, (src, dst) in enumerate(pairs)]
    for copy in copies:
        copy.start()
    for copy in copies:
        copy.wait()


def per_device(ZL, XY, tokens, slot_param, weight_in, weight_out, grad_out):
    _, patches, D = tokens.shape
    S = slot_param.shape[1]
    F = weight_in.shape[2]
    T = 2 * XY
    NZ = ZL * ZH
    rows = NZ * T
    PER = ZH * (D // LANES)
    DMA = pltpu.SemaphoreType.DMA
    vmem = pltpu.VMEM
    anywhere = pl.BlockSpec(memory_space=pl.ANY)
    in_hbm = pl.BlockSpec(memory_space=pltpu.HBM)
    in_vmem = pl.BlockSpec(memory_space=pltpu.VMEM)
    scratch = [
        vmem((patches, D), BF16), vmem((S, D), BF16), vmem((patches, D), BF16),
        vmem((2, D, F), BF16), vmem((2, F, D), BF16),
        vmem((patches, S), F32), vmem((patches, S), F32), vmem((patches, S), BF16), vmem((patches, S), BF16),
        vmem((2, T * PER, LANES), F32), vmem((2, T, PER, LANES), BF16), vmem((2, T, PER, LANES), BF16),
        vmem((ZH, 2, T, D), BF16), vmem((2, NZ, T, D), BF16),
        vmem((rows, F), F32), vmem((2, rows, F), F32), vmem((2, rows, F), BF16), vmem((2, rows, F), BF16),
        vmem((2, NZ, T, D), BF16), vmem((2, ZL + 2, T, D), BF16), vmem((2, 2, T, D), BF16), vmem((ZH, T, D), F32),
        vmem((2, T, PER, LANES), BF16), vmem((2, T, PER, LANES), BF16),
        vmem((2, S, D), BF16),
        vmem((2, D, F), BF16), vmem((2, F, D), BF16),
        vmem((T, 16, LANES), BF16), vmem((T, 16, LANES), BF16),
        vmem((16, LANES), BF16), vmem((NZ, 16, LANES), BF16),
        vmem((16, LANES), BF16), vmem((T, 16, LANES), BF16),
        DMA((5,)), DMA((2,)), DMA((2,)), DMA((2,)), DMA((2,)), DMA((2,)),
        DMA((2,)), DMA((2,)), DMA((2, 2)), DMA((2, 3)), DMA((2, 3)), DMA((2, 3)), DMA((2,)), DMA((2,)),
        DMA, DMA, DMA, DMA, DMA, DMA,
    ]
    shapes = (
        jax.ShapeDtypeStruct((patches, D), BF16),
        jax.ShapeDtypeStruct((S, D), F32),
        jax.ShapeDtypeStruct(weight_in.shape, BF16),
        jax.ShapeDtypeStruct(weight_out.shape, BF16),
    )
    results = pl.pallas_call(
        functools.partial(kernel, ZL, XY),
        out_shape=shapes,
        in_specs=[in_hbm] * 5,
        out_specs=[in_vmem, in_vmem, anywhere, anywhere],
        scratch_shapes=scratch,
        compiler_params=pltpu.CompilerParams(
            collective_id=0, has_side_effects=True, vmem_limit_bytes=40 * 1024 * 1024
        ),
    )(*(pltpu.with_memory_space_constraint(x, pltpu.HBM) for x in (tokens[0], slot_param.T, weight_in, weight_out, grad_out[0])))
    grad_tokens, grad_param, grad_win, grad_wout = pl.pallas_call(
        deliver,
        out_shape=shapes,
        in_specs=[anywhere] * 4,
        out_specs=[in_hbm] * 4,
        scratch_shapes=[DMA((4,))],
        compiler_params=pltpu.CompilerParams(vmem_limit_bytes=1024 * 1024),
    )(*results)
    return grad_tokens[None], grad_param.T, grad_win, grad_wout


def solution(mesh):
    ZL = mesh.shape["ex"] // 2
    XY = mesh.shape["ey"] // ZH
    split = Mesh(mesh.devices.reshape(ZL, 2, ZH, XY), AXES)
    return jax.shard_map(
        functools.partial(per_device, ZL, XY),
        mesh=split,
        in_specs=(P(ALL, None, None), P(), P(EY, None, EX), P(EY, EX, None), P(ALL, None, None)),
        out_specs=(P(ALL, None, None), P(), P(EY, None, EX), P(EY, EX, None)),
        check_vma=False,
    )
```

```python
import functools

import jax
import jax.numpy as jnp
from jax import lax
from jax.experimental import pallas as pl
from jax.experimental.pallas import tpu as pltpu
from jax.sharding import Mesh
from jax.sharding import PartitionSpec as P

AXES = ("zl", "core", "zh", "xy")
EX = ("zl", "core")
EY = ("zh", "xy")
ALL = AXES
ZH = 2
LANES = 128
F32 = jnp.float32
BF16 = jnp.bfloat16


def dot(a, b, ca, cb):
    return lax.dot_general(a, b, (((ca,), (cb,)), ((), ())), preferred_element_type=F32)


def softmax_along(values, axis):
    top = jnp.max(values, axis=axis, keepdims=True)
    expo = jnp.exp(values - top)
    return expo / jnp.sum(expo, axis=axis, keepdims=True)


def gelu_parts(pre):
    cdf = 0.5 * (1.0 + lax.erf(pre * 0.7071067811865476))
    slope = cdf + pre * jnp.exp(-0.5 * pre * pre) * 0.3989422804014327
    return (pre * cdf, slope)


def kernel(
    ZL, XY,
    tok_hbm, par_hbm, wi_hbm, wo_hbm, go_hbm,
    gt_out, gp_out, gwi_out, gwo_out,
    tok, par, go, wi, wo,
    disp, comb, disp_b, comb_b,
    rows32, send1, recv1, planes, gathered,
    pre_s, slope_s, hid, dpre,
    ysend, yin, ypair, fin, send2, recv2, slots,
    gwi_v, gwo_v,
    xsend, xrecv, zsend, zrecv, usend, urecv,
    in_sem, out_sem, w_send, w_recv, g_send, g_recv,
    a_send, a_recv, b_send, b_recv, y_send, y_recv, c_send, c_recv,
    x_send, x_recv, z_send, z_recv, u_send, u_recv,
):
    T = 2 * XY
    NZ = ZL * ZH
    S, D = par.shape
    J = D // LANES
    zl = lax.axis_index("zl")
    core = lax.axis_index("core")
    zh = lax.axis_index("zh")
    xy = lax.axis_index("xy")
    me_t = xy * 2 + core
    me_z = zh * ZL + zl

    def in_plane(d):
        t = lax.rem(me_t + 11 * d, T)
        return t, (zl, lax.rem(t, 2), zh, lax.div(t, 2))

    def along_z(d):
        z = lax.rem(me_z + d, NZ)
        return z, (lax.rem(z, ZL), core, lax.div(z, ZL), xy)

    sibling = (zl, 1 - core, zh, xy)

    def remote(src, dst, send_sem, recv_sem, device):
        return pltpu.make_async_remote_copy(
            src_ref=src, dst_ref=dst, send_sem=send_sem, recv_sem=recv_sem,
            device_id=device, device_id_type=pl.DeviceIdType.MESH,
        )

    barrier = pltpu.get_barrier_semaphore()

    def greet_plane(d, carry):
        pl.semaphore_signal(barrier, inc=1, device_id=in_plane(d)[1], device_id_type=pl.DeviceIdType.MESH)
        return carry

    def greet_z(d, carry):
        pl.semaphore_signal(barrier, inc=1, device_id=along_z(d)[1], device_id_type=pl.DeviceIdType.MESH)
        return carry

    loads = [
        pltpu.make_async_copy(tok_hbm, tok, in_sem.at[0]),
        pltpu.make_async_copy(par_hbm, par, in_sem.at[1]),
        pltpu.make_async_copy(go_hbm, go, in_sem.at[2]),
        pltpu.make_async_copy(wi_hbm.at[core], wi.at[core], in_sem.at[3]),
        pltpu.make_async_copy(wo_hbm.at[core], wo.at[core], in_sem.at[4]),
    ]
    for load in loads:
        load.start()
    lax.fori_loop(1, T, greet_plane, 0)
    lax.fori_loop(1, NZ, greet_z, 0)

    def pack(part, h, w):
        for j in range(J):
            rows32[w, pl.ds(h * J + j, T, stride=ZH * J), :] = part[:, j * LANES : (j + 1) * LANES]

    def messages(w):
        return rows32[w].reshape(T, ZH * J, LANES).astype(BF16)

    def unpack(h, w, j):
        return rows32[w, pl.ds(h * J + j, T, stride=ZH * J), :].astype(BF16)

    def arrived(send, recv, w):
        recv[w, me_t] = send[w, me_t]
        rows32[w] = recv[w].reshape(T * ZH * J, LANES).astype(F32)

    def all_to_all(send, recv, send_sem, recv_sem):
        def go_to(d, carry):
            t, device = in_plane(d)
            remote(send.at[t], recv.at[me_t], send_sem, recv_sem, device).start()
            return carry

        lax.fori_loop(1, T, go_to, 0)

    def wait_for(ref, sem):
        pltpu.make_async_copy(ref, ref, sem).wait()

    def wait_all(ref, count, sem):
        wait_for(ref.at[pl.ds(0, count)], sem)

    loads[0].wait()
    loads[1].wait()
    logits = dot(tok[...], par[...], 1, 1)
    dispatch = softmax_along(logits, 0)
    disp[...] = dispatch
    disp_b[...] = dispatch.astype(BF16)
    slot_in = dot(disp_b[...], tok[...], 0, 0)
    for h in range(ZH):
        pack(slot_in[h * T : (h + 1) * T], h, 0)
    send1[0] = messages(0)
    pl.semaphore_wait(barrier, T - 1 + NZ - 1)
    all_to_all(send1.at[0], recv1.at[0], a_send.at[0], a_recv.at[0])
    combine = softmax_along(logits, 1)
    comb[...] = combine
    comb_b[...] = combine.astype(BF16)
    loads[2].wait()
    slot_cot = dot(comb_b[...], go[...], 0, 0)
    for h in range(ZH):
        pack(slot_cot[h * T : (h + 1) * T], h, 1)
    send1[1] = messages(1)
    all_to_all(send1.at[1], recv1.at[1], a_send.at[1], a_recv.at[1])
    swap = [
        remote(wi_hbm.at[1 - core], wi.at[core], w_send.at[0], w_recv.at[0], sibling),
        remote(wo_hbm.at[1 - core], wo.at[core], w_send.at[1], w_recv.at[1], sibling),
    ]
    for copy in swap:
        copy.start()

    odd = lax.rem(zl, 2)
    partner = (zl + 1 - 2 * odd, core, zh, xy)
    mine = (1 - zh) * ZL + 2 * (1 - odd)
    theirs = (1 - zh) * ZL + 2 * odd

    def in_group(d):
        k = lax.rem(zl + d, ZL)
        return zh * ZL + k, (k, core, zh, xy)

    def send_planes(w):
        wait_all(send1.at[w], T - 1, a_send.at[w])
        wait_all(recv1.at[w], T - 1, a_recv.at[w])
        arrived(send1, recv1, w)
        for h in range(ZH):
            for j in range(J):
                planes[h, w, :, j * LANES : (j + 1) * LANES] = unpack(h, w, j)
        device = (3 * (1 - lax.div(zl, 2)), core, 1 - zh, xy)
        remote(planes.at[1 - zh, w], gathered.at[w, me_z], b_send.at[w], b_recv.at[w, ZL + lax.div(zl, 2)], device).start()
        for d in (2, 1, 3):

            @pl.when(zl != {1: ZL - 1, 2: ZL, 3: 0}[d])
            def _(d=d):
                remote(planes.at[zh, w], gathered.at[w, me_z], b_send.at[w], b_recv.at[w, zl], in_group(d)[1]).start()

        gathered[w, me_z] = planes[zh, w]

    def own(w, k):
        return gathered.at[w, zh * ZL + k]

    def pair(w, k):
        return gathered.at[w, pl.ds((1 - zh) * ZL + 2 * k, 2)]

    def to_place(block, w, sem, k):
        remote(block, block, b_send.at[w], b_recv.at[w, sem], (k, core, zh, xy)).start()

    def take_own(w, k):
        wait_for(own(w, k), b_recv.at[w, k])

    def take_pair(w, k):
        wait_for(pair(w, k), b_recv.at[w, ZL + k])

    def pass_on(w):
        @pl.when(zl == 0)
        def _():
            take_pair(w, 1)
            to_place(pair(w, 1), w, ZL + 1, 2)
            to_place(pair(w, 1), w, ZL + 1, 1)

        @pl.when(zl == 3)
        def _():
            take_pair(w, 0)
            to_place(pair(w, 0), w, ZL, 1)
            to_place(pair(w, 0), w, ZL, 2)

        @pl.when(zl == 1)
        def _():
            take_own(w, 3)
            to_place(own(w, 3), w, 3, 0)
            take_pair(w, 0)
            to_place(pair(w, 0), w, ZL, 0)

        @pl.when(zl == 2)
        def _():
            take_own(w, 0)
            to_place(own(w, 0), w, 0, 3)
            take_pair(w, 1)
            to_place(pair(w, 1), w, ZL + 1, 3)

    def all_here(w):
        for p, left, last in ((0, (1, 2, 3), 0), (1, (0, 2), 1), (2, (1, 3), 0), (3, (0, 1, 2), 1)):

            @pl.when(zl == p)
            def _(left=left, last=last):
                for k in left:
                    take_own(w, k)
                take_pair(w, last)

    def send_back(w):
        remote(ysend.at[w, pl.ds(theirs, 2)], ypair.at[w], y_send.at[w, 1], y_recv.at[w, 1], partner).start()
        for d in (2, 1, 3):
            z, device = in_group(d)
            remote(ysend.at[w, z], yin.at[w, zl], y_send.at[w, 0], y_recv.at[w, 0], device).start()
        yin[w, zl] = ysend[w, me_z]

    def send_pairs(w):
        wait_for(ypair.at[w], y_recv.at[w, 1])
        for k in range(2):
            ysend[w, mine + k] = (ysend[w, mine + k].astype(F32) + ypair[w, k].astype(F32)).astype(BF16)
            device = (2 * (1 - odd) + k, core, 1 - zh, xy)
            remote(ysend.at[w, mine + k], yin.at[w, ZL + lax.div(zl, 2)], y_send.at[w, 2], y_recv.at[w, 2], device).start()

    def sums_back(w):
        wait_for(yin.at[w, pl.ds(0, ZL - 1)], y_recv.at[w, 0])
        wait_for(yin.at[w, pl.ds(ZL, 2)], y_recv.at[w, 2])
        fin[zh] = jnp.sum(yin[w, :ZL].astype(F32), axis=0)
        fin[1 - zh] = yin[w, ZL].astype(F32) + yin[w, ZL + 1].astype(F32)
        for h in range(ZH):
            pack(fin[h], h, w)
        send2[w] = messages(w)
        all_to_all(send2.at[w], recv2.at[w], c_send.at[w], c_recv.at[w])

    def take_slots(w):
        wait_all(recv2.at[w], T - 1, c_recv.at[w])
        arrived(send2, recv2, w)
        for h in range(ZH):
            for j in range(J):
                slots[w, h * T : (h + 1) * T, j * LANES : (j + 1) * LANES] = unpack(h, w, j)

    send_planes(0)
    send_planes(1)
    for copy in loads[3:] + swap:
        copy.wait()
    pass_on(0)

    rows = NZ * T
    step = min(16, rows)

    def by_rows(body):
        def one(k, carry):
            body(pl.ds(pl.multiple_of(k * step, step), step))
            return carry

        lax.fori_loop(0, rows // step, one, 0)

    def whole(w):
        return gathered[w].reshape(rows, D)

    def pre_part(f):
        pre_s[...] = dot(whole(0), wi[f], 1, 0)

        def body(part):
            value, slope = gelu_parts(pre_s[part, :])
            hid[f, part, :] = value.astype(BF16)
            slope_s[f, part, :] = slope

        by_rows(body)

    def back_part(f):
        pre_s[...] = dot(whole(1), wo[f], 1, 1)

        def body(part):
            dpre[f, part, :] = (pre_s[part, :] * slope_s[f, part, :]).astype(BF16)

        by_rows(body)

    def out_part(w):
        if w == 0:
            total = dot(hid[0], wo[0], 1, 0) + dot(hid[1], wo[1], 1, 0)
        else:
            total = dot(dpre[0], wi[0], 1, 1) + dot(dpre[1], wi[1], 1, 1)
        ysend[w] = total.astype(BF16).reshape(ysend.shape[1:])

    def win_part(f):
        gwi_v[f] = dot(whole(0), dpre[f], 0, 0).astype(BF16)

    def wout_part(f):
        gwo_v[f] = dot(hid[f], whole(1), 0, 0).astype(BF16)

    pass_on(1)
    all_here(0)
    pre_part(0)
    pre_part(1)
    out_part(0)
    send_back(0)
    all_here(1)
    back_part(0)
    send_pairs(0)
    back_part(1)
    out_part(1)
    send_back(1)
    for f in range(2):
        wout_part(f)
    send_pairs(1)
    for f in range(2):
        win_part(f)
    stores = [
        pltpu.make_async_copy(gwi_v.at[core], gwi_out.at[core], out_sem.at[0]),
        pltpu.make_async_copy(gwo_v.at[core], gwo_out.at[core], out_sem.at[1]),
        remote(gwi_v.at[1 - core], gwi_out.at[core], g_send.at[0], g_recv.at[0], sibling),
        remote(gwo_v.at[1 - core], gwo_out.at[core], g_send.at[1], g_recv.at[1], sibling),
    ]
    for copy in stores:
        copy.start()

    sums_back(0)
    take_slots(0)
    d_combine = dot(go[...], slots[0], 1, 1)
    combine = comb[...]
    by_combine = combine * (d_combine - jnp.sum(combine * d_combine, axis=1, keepdims=True))
    sums_back(1)
    for w in range(2):
        wait_all(gathered.at[w], 7, b_send.at[w])
        wait_all(ysend.at[w], ZL - 1, y_send.at[w, 0])
        wait_all(ysend.at[w], 2, y_send.at[w, 1])
        wait_all(ysend.at[w], 2, y_send.at[w, 2])
        wait_all(send2.at[w], T - 1, c_send.at[w])
    take_slots(1)
    d_dispatch = dot(tok[...], slots[1], 1, 1)
    dispatch = disp[...]
    d_logits = dispatch * (d_dispatch - jnp.sum(dispatch * d_dispatch, axis=0, keepdims=True))
    d_logits = d_logits + by_combine
    logit_grad = d_logits.astype(BF16)
    local_param = dot(logit_grad, tok[...], 0, 0)

    R = min(16, S)
    tiles = [
        (k * R // 16, slice(k * R % 16, k * R % 16 + R), slice(r, r + R), slice(j * LANES, (j + 1) * LANES))
        for k, (r, j) in enumerate((r, j) for r in range(0, S, R) for j in range(J))
    ]
    for k, inside, row, column in tiles:
        xsend[k, inside, :] = local_param[row, column].astype(BF16)
    all_to_all(xsend, xrecv, x_send, x_recv)
    gt_out[...] = (dot(disp_b[...], slots[1], 1, 0) + dot(logit_grad, par[...], 1, 0)).astype(BF16)
    wait_all(xsend, T - 1, x_send)
    wait_all(xrecv, T - 1, x_recv)
    xrecv[me_t] = xsend[me_t]
    zsend[...] = jnp.sum(xrecv[...].astype(F32), axis=0).astype(BF16)

    def send_sum(d, carry):
        remote(zsend, zrecv.at[me_z], z_send, z_recv, along_z(d)[1]).start()
        return carry

    lax.fori_loop(1, NZ, send_sum, 0)
    wait_all(zrecv, NZ - 1, z_send)
    wait_all(zrecv, NZ - 1, z_recv)
    zrecv[me_z] = zsend[...]
    usend[...] = jnp.sum(zrecv[...].astype(F32), axis=0).astype(BF16)

    def send_total(d, carry):
        remote(usend, urecv.at[me_t], u_send, u_recv, in_plane(d)[1]).start()
        return carry

    lax.fori_loop(1, T, send_total, 0)
    wait_all(urecv, T - 1, u_send)
    wait_all(urecv, T - 1, u_recv)
    urecv[me_t] = usend[...]
    for k, inside, row, column in tiles:
        gp_out[row, column] = urecv[k, inside, :].astype(F32)
    for copy in stores:
        copy.wait()


def deliver(gt, gp, gwi, gwo, gt_out, gp_out, gwi_out, gwo_out, sem):
    pairs = [(gt, gt_out), (gp, gp_out)]
    for src, dst in ((gwi, gwi_out), (gwo, gwo_out)):
        rows = src.shape[1] // 4
        for part in range(8):
            at = (part // 4, pl.ds(part % 4 * rows, rows))
            pairs.append((src.at[at], dst.at[at]))
    copies = [pltpu.make_async_copy(src, dst, sem.at[k]) for k, (src, dst) in enumerate(pairs)]
    for copy in copies:
        copy.start()
    for copy in copies:
        copy.wait()


def per_device(ZL, XY, tokens, slot_param, weight_in, weight_out, grad_out):
    _, patches, D = tokens.shape
    S = slot_param.shape[1]
    F = weight_in.shape[2]
    T = 2 * XY
    NZ = ZL * ZH
    rows = NZ * T
    PER = ZH * (D // LANES)
    DMA = pltpu.SemaphoreType.DMA
    vmem = pltpu.VMEM
    anywhere = pl.BlockSpec(memory_space=pl.ANY)
    in_hbm = pl.BlockSpec(memory_space=pltpu.HBM)
    in_vmem = pl.BlockSpec(memory_space=pltpu.VMEM)
    scratch = [
        vmem((patches, D), BF16), vmem((S, D), BF16), vmem((patches, D), BF16),
        vmem((2, D, F), BF16), vmem((2, F, D), BF16),
        vmem((patches, S), F32), vmem((patches, S), F32), vmem((patches, S), BF16), vmem((patches, S), BF16),
        vmem((2, T * PER, LANES), F32), vmem((2, T, PER, LANES), BF16), vmem((2, T, PER, LANES), BF16),
        vmem((ZH, 2, T, D), BF16), vmem((2, NZ, T, D), BF16),
        vmem((rows, F), F32), vmem((2, rows, F), F32), vmem((2, rows, F), BF16), vmem((2, rows, F), BF16),
        vmem((2, NZ, T, D), BF16), vmem((2, ZL + 2, T, D), BF16), vmem((2, 2, T, D), BF16), vmem((ZH, T, D), F32),
        vmem((2, T, PER, LANES), BF16), vmem((2, T, PER, LANES), BF16),
        vmem((2, S, D), BF16),
        vmem((2, D, F), BF16), vmem((2, F, D), BF16),
        vmem((T, 16, LANES), BF16), vmem((T, 16, LANES), BF16),
        vmem((16, LANES), BF16), vmem((NZ, 16, LANES), BF16),
        vmem((16, LANES), BF16), vmem((T, 16, LANES), BF16),
        DMA((5,)), DMA((2,)), DMA((2,)), DMA((2,)), DMA((2,)), DMA((2,)),
        DMA((2,)), DMA((2,)), DMA((2,)), DMA((2, ZL + 2)), DMA((2, 3)), DMA((2, 3)), DMA((2,)), DMA((2,)),
        DMA, DMA, DMA, DMA, DMA, DMA,
    ]
    shapes = (
        jax.ShapeDtypeStruct((patches, D), BF16),
        jax.ShapeDtypeStruct((S, D), F32),
        jax.ShapeDtypeStruct(weight_in.shape, BF16),
        jax.ShapeDtypeStruct(weight_out.shape, BF16),
    )
    results = pl.pallas_call(
        functools.partial(kernel, ZL, XY),
        out_shape=shapes,
        in_specs=[in_hbm] * 5,
        out_specs=[in_vmem, in_vmem, anywhere, anywhere],
        scratch_shapes=scratch,
        compiler_params=pltpu.CompilerParams(
            collective_id=0, has_side_effects=True, vmem_limit_bytes=40 * 1024 * 1024
        ),
    )(*(pltpu.with_memory_space_constraint(x, pltpu.HBM) for x in (tokens[0], slot_param.T, weight_in, weight_out, grad_out[0])))
    grad_tokens, grad_param, grad_win, grad_wout = pl.pallas_call(
        deliver,
        out_shape=shapes,
        in_specs=[anywhere] * 4,
        out_specs=[in_hbm] * 4,
        scratch_shapes=[DMA((18,))],
        compiler_params=pltpu.CompilerParams(vmem_limit_bytes=1024 * 1024),
    )(*results)
    return grad_tokens[None], grad_param.T, grad_win, grad_wout


def solution(mesh):
    ZL = mesh.shape["ex"] // 2
    XY = mesh.shape["ey"] // ZH
    split = Mesh(mesh.devices.reshape(ZL, 2, ZH, XY), AXES)
    return jax.shard_map(
        functools.partial(per_device, ZL, XY),
        mesh=split,
        in_specs=(P(ALL, None, None), P(), P(EY, None, EX), P(EY, EX, None), P(ALL, None, None)),
        out_specs=(P(ALL, None, None), P(), P(EY, None, EX), P(EY, EX, None)),
        check_vma=False,
    )
```

```python
import functools

import jax
import jax.numpy as jnp
from jax import lax
from jax.experimental import pallas as pl
from jax.experimental.pallas import tpu as pltpu
from jax.sharding import Mesh
from jax.sharding import PartitionSpec as P

AXES = ("zl", "core", "zh", "xy")
EX = ("zl", "core")
EY = ("zh", "xy")
ALL = AXES
ZH = 2
LANES = 128
F32 = jnp.float32
BF16 = jnp.bfloat16


def dot(a, b, ca, cb):
    return lax.dot_general(a, b, (((ca,), (cb,)), ((), ())), preferred_element_type=F32)


def softmax_along(values, axis):
    top = jnp.max(values, axis=axis, keepdims=True)
    expo = jnp.exp(values - top)
    return expo / jnp.sum(expo, axis=axis, keepdims=True)


def gelu_parts(pre):
    cdf = 0.5 * (1.0 + lax.erf(pre * 0.7071067811865476))
    slope = cdf + pre * jnp.exp(-0.5 * pre * pre) * 0.3989422804014327
    return (pre * cdf, slope)


def kernel(
    ZL, XY,
    tok_hbm, par_hbm, wi_hbm, wo_hbm, go_hbm,
    gt_out, gp_out, gwi_out, gwo_out,
    tok, par, go, wi, wo,
    disp, comb, disp_b, comb_b,
    rows32, send1, recv1, planes, gathered,
    pre_s, slope_s, hid, dpre,
    ysend, yin, ypair, fin, send2, recv2, slots,
    gwi_v, gwo_v,
    xsend, xrecv, zsend, zrecv, usend, urecv,
    in_sem, out_sem, w_send, w_recv, g_send, g_recv,
    a_send, a_recv, b_send, b_recv, y_send, y_recv, c_send, c_recv,
    x_send, x_recv, z_send, z_recv, u_send, u_recv,
):
    T = 2 * XY
    NZ = ZL * ZH
    S, D = par.shape
    J = D // LANES
    zl = lax.axis_index("zl")
    core = lax.axis_index("core")
    zh = lax.axis_index("zh")
    xy = lax.axis_index("xy")
    me_t = xy * 2 + core
    me_z = zh * ZL + zl

    def in_plane(d):
        t = lax.rem(me_t + 11 * d, T)
        return t, (zl, lax.rem(t, 2), zh, lax.div(t, 2))

    def along_z(d):
        z = lax.rem(me_z + d, NZ)
        return z, (lax.rem(z, ZL), core, lax.div(z, ZL), xy)

    sibling = (zl, 1 - core, zh, xy)

    def remote(src, dst, send_sem, recv_sem, device):
        return pltpu.make_async_remote_copy(
            src_ref=src, dst_ref=dst, send_sem=send_sem, recv_sem=recv_sem,
            device_id=device, device_id_type=pl.DeviceIdType.MESH,
        )

    barrier = pltpu.get_barrier_semaphore()

    def greet_plane(d, carry):
        pl.semaphore_signal(barrier, inc=1, device_id=in_plane(d)[1], device_id_type=pl.DeviceIdType.MESH)
        return carry

    def greet_z(d, carry):
        pl.semaphore_signal(barrier, inc=1, device_id=along_z(d)[1], device_id_type=pl.DeviceIdType.MESH)
        return carry

    loads = [
        pltpu.make_async_copy(tok_hbm, tok, in_sem.at[0]),
        pltpu.make_async_copy(par_hbm, par, in_sem.at[1]),
        pltpu.make_async_copy(go_hbm, go, in_sem.at[2]),
        pltpu.make_async_copy(wi_hbm.at[core], wi.at[core], in_sem.at[3]),
        pltpu.make_async_copy(wo_hbm.at[core], wo.at[core], in_sem.at[4]),
    ]
    for load in loads:
        load.start()
    lax.fori_loop(1, T, greet_plane, 0)
    lax.fori_loop(1, NZ, greet_z, 0)

    def pack(part, h, w):
        for j in range(J):
            rows32[w, pl.ds(h * J + j, T, stride=ZH * J), :] = part[:, j * LANES : (j + 1) * LANES]

    def messages(w):
        return rows32[w].reshape(T, ZH * J, LANES).astype(BF16)

    def unpack(h, w, j):
        return rows32[w, pl.ds(h * J + j, T, stride=ZH * J), :].astype(BF16)

    def arrived(send, recv, w):
        recv[w, me_t] = send[w, me_t]
        rows32[w] = recv[w].reshape(T * ZH * J, LANES).astype(F32)

    def all_to_all(send, recv, send_sem, recv_sem):
        def go_to(d, carry):
            t, device = in_plane(d)
            remote(send.at[t], recv.at[me_t], send_sem, recv_sem, device).start()
            return carry

        lax.fori_loop(1, T, go_to, 0)

    def wait_for(ref, sem):
        pltpu.make_async_copy(ref, ref, sem).wait()

    def wait_all(ref, count, sem):
        wait_for(ref.at[pl.ds(0, count)], sem)

    loads[0].wait()
    loads[1].wait()
    logits = dot(tok[...], par[...], 1, 1)
    dispatch = softmax_along(logits, 0)
    disp[...] = dispatch
    disp_b[...] = dispatch.astype(BF16)
    slot_in = dot(disp_b[...], tok[...], 0, 0)
    for h in range(ZH):
        pack(slot_in[h * T : (h + 1) * T], h, 0)
    send1[0] = messages(0)
    pl.semaphore_wait(barrier, T - 1 + NZ - 1)
    all_to_all(send1.at[0], recv1.at[0], a_send.at[0], a_recv.at[0])
    combine = softmax_along(logits, 1)
    comb[...] = combine
    comb_b[...] = combine.astype(BF16)
    loads[2].wait()
    slot_cot = dot(comb_b[...], go[...], 0, 0)
    for h in range(ZH):
        pack(slot_cot[h * T : (h + 1) * T], h, 1)
    send1[1] = messages(1)
    all_to_all(send1.at[1], recv1.at[1], a_send.at[1], a_recv.at[1])
    swap = [
        remote(wi_hbm.at[1 - core], wi.at[core], w_send.at[0], w_recv.at[0], sibling),
        remote(wo_hbm.at[1 - core], wo.at[core], w_send.at[1], w_recv.at[1], sibling),
    ]
    for copy in swap:
        copy.start()

    odd = lax.rem(zl, 2)
    partner = (zl + 1 - 2 * odd, core, zh, xy)
    mine = (1 - zh) * ZL + 2 * (1 - odd)
    theirs = (1 - zh) * ZL + 2 * odd

    def in_group(d):
        k = lax.rem(zl + d, ZL)
        return zh * ZL + k, (k, core, zh, xy)

    def send_planes(w):
        wait_all(send1.at[w], T - 1, a_send.at[w])
        wait_all(recv1.at[w], T - 1, a_recv.at[w])
        arrived(send1, recv1, w)
        for h in range(ZH):
            for j in range(J):
                planes[h, w, :, j * LANES : (j + 1) * LANES] = unpack(h, w, j)
        device = (3 * (1 - lax.div(zl, 2)), core, 1 - zh, xy)
        remote(planes.at[1 - zh, w], gathered.at[w, me_z], b_send.at[w], b_recv.at[w, ZL + lax.div(zl, 2)], device).start()
        for d in (2, 1, 3):

            @pl.when(zl != {1: ZL - 1, 2: ZL, 3: 0}[d])
            def _(d=d):
                remote(planes.at[zh, w], gathered.at[w, me_z], b_send.at[w], b_recv.at[w, zl], in_group(d)[1]).start()

        gathered[w, me_z] = planes[zh, w]

    def own(w, k):
        return gathered.at[w, zh * ZL + k]

    def pair(w, k):
        return gathered.at[w, pl.ds((1 - zh) * ZL + 2 * k, 2)]

    def to_place(block, w, sem, k):
        remote(block, block, b_send.at[w], b_recv.at[w, sem], (k, core, zh, xy)).start()

    def take_own(w, k):
        wait_for(own(w, k), b_recv.at[w, k])

    def take_pair(w, k):
        wait_for(pair(w, k), b_recv.at[w, ZL + k])

    def pass_on(w):
        @pl.when(zl == 0)
        def _():
            take_pair(w, 1)
            to_place(pair(w, 1), w, ZL + 1, 2)
            to_place(pair(w, 1), w, ZL + 1, 1)

        @pl.when(zl == 3)
        def _():
            take_pair(w, 0)
            to_place(pair(w, 0), w, ZL, 1)
            to_place(pair(w, 0), w, ZL, 2)

        @pl.when(zl == 1)
        def _():
            take_own(w, 3)
            to_place(own(w, 3), w, 3, 0)
            take_pair(w, 0)
            to_place(pair(w, 0), w, ZL, 0)

        @pl.when(zl == 2)
        def _():
            take_own(w, 0)
            to_place(own(w, 0), w, 0, 3)
            take_pair(w, 1)
            to_place(pair(w, 1), w, ZL + 1, 3)

    def all_here(w):
        for p, left, last in ((0, (1, 2, 3), 0), (1, (0, 2), 1), (2, (1, 3), 0), (3, (0, 1, 2), 1)):

            @pl.when(zl == p)
            def _(left=left, last=last):
                for k in left:
                    take_own(w, k)
                take_pair(w, last)

    def send_back(w):
        remote(ysend.at[w, pl.ds(theirs, 2)], ypair.at[w], y_send.at[w, 1], y_recv.at[w, 1], partner).start()
        for d in (2, 1, 3):
            z, device = in_group(d)
            remote(ysend.at[w, z], yin.at[w, zl], y_send.at[w, 0], y_recv.at[w, 0], device).start()
        yin[w, zl] = ysend[w, me_z]

    def send_pairs(w):
        wait_for(ypair.at[w], y_recv.at[w, 1])
        for k in range(2):
            ysend[w, mine + k] = (ysend[w, mine + k].astype(F32) + ypair[w, k].astype(F32)).astype(BF16)
            device = (2 * (1 - odd) + k, core, 1 - zh, xy)
            remote(ysend.at[w, mine + k], yin.at[w, ZL + lax.div(zl, 2)], y_send.at[w, 2], y_recv.at[w, 2], device).start()

    def sums_back(w):
        wait_for(yin.at[w, pl.ds(0, ZL - 1)], y_recv.at[w, 0])
        wait_for(yin.at[w, pl.ds(ZL, 2)], y_recv.at[w, 2])
        fin[zh] = jnp.sum(yin[w, :ZL].astype(F32), axis=0)
        fin[1 - zh] = yin[w, ZL].astype(F32) + yin[w, ZL + 1].astype(F32)
        for h in range(ZH):
            pack(fin[h], h, w)
        send2[w] = messages(w)
        all_to_all(send2.at[w], recv2.at[w], c_send.at[w], c_recv.at[w])

    def take_slots(w):
        wait_all(recv2.at[w], T - 1, c_recv.at[w])
        arrived(send2, recv2, w)
        for h in range(ZH):
            for j in range(J):
                slots[w, h * T : (h + 1) * T, j * LANES : (j + 1) * LANES] = unpack(h, w, j)

    send_planes(0)
    send_planes(1)
    pass_on(0)

    rows = NZ * T
    step = min(16, rows)

    def by_rows(body):
        def one(k, carry):
            body(pl.ds(pl.multiple_of(k * step, step), step))
            return carry

        lax.fori_loop(0, rows // step, one, 0)

    def whole(w):
        return gathered[w].reshape(rows, D)

    def pre_part(f):
        pre_s[...] = dot(whole(0), wi[f], 1, 0)

        def body(part):
            value, slope = gelu_parts(pre_s[part, :])
            hid[f, part, :] = value.astype(BF16)
            slope_s[f, part, :] = slope

        by_rows(body)

    def back_part(f):
        pre_s[...] = dot(whole(1), wo[f], 1, 1)

        def body(part):
            dpre[f, part, :] = (pre_s[part, :] * slope_s[f, part, :]).astype(BF16)

        by_rows(body)

    def out_part(w):
        if w == 0:
            total = dot(hid[0], wo[0], 1, 0) + dot(hid[1], wo[1], 1, 0)
        else:
            total = dot(dpre[0], wi[0], 1, 1) + dot(dpre[1], wi[1], 1, 1)
        ysend[w] = total.astype(BF16).reshape(ysend.shape[1:])

    def win_part(f):
        gwi_v[f] = dot(whole(0), dpre[f], 0, 0).astype(BF16)

    def wout_part(f):
        gwo_v[f] = dot(hid[f], whole(1), 0, 0).astype(BF16)

    pass_on(1)
    all_here(0)
    for copy in loads[3:] + swap:
        copy.wait()
    pre_part(0)
    pre_part(1)
    out_part(0)
    send_back(0)
    all_here(1)
    back_part(0)
    send_pairs(0)
    back_part(1)
    out_part(1)
    send_back(1)
    for f in range(2):
        wout_part(f)
    send_pairs(1)
    for f in range(2):
        win_part(f)
    stores = [
        pltpu.make_async_copy(gwi_v.at[core], gwi_out.at[core], out_sem.at[0]),
        pltpu.make_async_copy(gwo_v.at[core], gwo_out.at[core], out_sem.at[1]),
        remote(gwi_v.at[1 - core], gwi_out.at[core], g_send.at[0], g_recv.at[0], sibling),
        remote(gwo_v.at[1 - core], gwo_out.at[core], g_send.at[1], g_recv.at[1], sibling),
    ]
    for copy in stores:
        copy.start()

    sums_back(0)
    take_slots(0)
    d_combine = dot(go[...], slots[0], 1, 1)
    combine = comb[...]
    by_combine = combine * (d_combine - jnp.sum(combine * d_combine, axis=1, keepdims=True))
    sums_back(1)
    for w in range(2):
        wait_all(gathered.at[w], 7, b_send.at[w])
        wait_all(ysend.at[w], ZL - 1, y_send.at[w, 0])
        wait_all(ysend.at[w], 2, y_send.at[w, 1])
        wait_all(ysend.at[w], 2, y_send.at[w, 2])
        wait_all(send2.at[w], T - 1, c_send.at[w])
    take_slots(1)
    d_dispatch = dot(tok[...], slots[1], 1, 1)
    dispatch = disp[...]
    d_logits = dispatch * (d_dispatch - jnp.sum(dispatch * d_dispatch, axis=0, keepdims=True))
    d_logits = d_logits + by_combine
    logit_grad = d_logits.astype(BF16)
    local_param = dot(logit_grad, tok[...], 0, 0)

    R = min(16, S)
    tiles = [
        (k * R // 16, slice(k * R % 16, k * R % 16 + R), slice(r, r + R), slice(j * LANES, (j + 1) * LANES))
        for k, (r, j) in enumerate((r, j) for r in range(0, S, R) for j in range(J))
    ]
    for k, inside, row, column in tiles:
        xsend[k, inside, :] = local_param[row, column].astype(BF16)
    all_to_all(xsend, xrecv, x_send, x_recv)
    gt_out[...] = (dot(disp_b[...], slots[1], 1, 0) + dot(logit_grad, par[...], 1, 0)).astype(BF16)
    wait_all(xsend, T - 1, x_send)
    wait_all(xrecv, T - 1, x_recv)
    xrecv[me_t] = xsend[me_t]
    zsend[...] = jnp.sum(xrecv[...].astype(F32), axis=0).astype(BF16)

    def send_sum(d, carry):
        remote(zsend, zrecv.at[me_z], z_send, z_recv, along_z(d)[1]).start()
        return carry

    lax.fori_loop(1, NZ, send_sum, 0)
    wait_all(zrecv, NZ - 1, z_send)
    wait_all(zrecv, NZ - 1, z_recv)
    zrecv[me_z] = zsend[...]
    usend[...] = jnp.sum(zrecv[...].astype(F32), axis=0).astype(BF16)

    def send_total(d, carry):
        remote(usend, urecv.at[me_t], u_send, u_recv, in_plane(d)[1]).start()
        return carry

    lax.fori_loop(1, T, send_total, 0)
    wait_all(urecv, T - 1, u_send)
    wait_all(urecv, T - 1, u_recv)
    urecv[me_t] = usend[...]
    for k, inside, row, column in tiles:
        gp_out[row, column] = urecv[k, inside, :].astype(F32)
    for copy in stores:
        copy.wait()


def deliver(gt, gp, gwi, gwo, gt_out, gp_out, gwi_out, gwo_out, sem):
    pairs = [(gt, gt_out), (gp, gp_out)]
    for src, dst in ((gwi, gwi_out), (gwo, gwo_out)):
        rows = src.shape[1] // 4
        for part in range(8):
            at = (part // 4, pl.ds(part % 4 * rows, rows))
            pairs.append((src.at[at], dst.at[at]))
    copies = [pltpu.make_async_copy(src, dst, sem.at[k]) for k, (src, dst) in enumerate(pairs)]
    for copy in copies:
        copy.start()
    for copy in copies:
        copy.wait()


def per_device(ZL, XY, tokens, slot_param, weight_in, weight_out, grad_out):
    _, patches, D = tokens.shape
    S = slot_param.shape[1]
    F = weight_in.shape[2]
    T = 2 * XY
    NZ = ZL * ZH
    rows = NZ * T
    PER = ZH * (D // LANES)
    DMA = pltpu.SemaphoreType.DMA
    vmem = pltpu.VMEM
    anywhere = pl.BlockSpec(memory_space=pl.ANY)
    in_hbm = pl.BlockSpec(memory_space=pltpu.HBM)
    in_vmem = pl.BlockSpec(memory_space=pltpu.VMEM)
    scratch = [
        vmem((patches, D), BF16), vmem((S, D), BF16), vmem((patches, D), BF16),
        vmem((2, D, F), BF16), vmem((2, F, D), BF16),
        vmem((patches, S), F32), vmem((patches, S), F32), vmem((patches, S), BF16), vmem((patches, S), BF16),
        vmem((2, T * PER, LANES), F32), vmem((2, T, PER, LANES), BF16), vmem((2, T, PER, LANES), BF16),
        vmem((ZH, 2, T, D), BF16), vmem((2, NZ, T, D), BF16),
        vmem((rows, F), F32), vmem((2, rows, F), F32), vmem((2, rows, F), BF16), vmem((2, rows, F), BF16),
        vmem((2, NZ, T, D), BF16), vmem((2, ZL + 2, T, D), BF16), vmem((2, 2, T, D), BF16), vmem((ZH, T, D), F32),
        vmem((2, T, PER, LANES), BF16), vmem((2, T, PER, LANES), BF16),
        vmem((2, S, D), BF16),
        vmem((2, D, F), BF16), vmem((2, F, D), BF16),
        vmem((T, 16, LANES), BF16), vmem((T, 16, LANES), BF16),
        vmem((16, LANES), BF16), vmem((NZ, 16, LANES), BF16),
        vmem((16, LANES), BF16), vmem((T, 16, LANES), BF16),
        DMA((5,)), DMA((2,)), DMA((2,)), DMA((2,)), DMA((2,)), DMA((2,)),
        DMA((2,)), DMA((2,)), DMA((2,)), DMA((2, ZL + 2)), DMA((2, 3)), DMA((2, 3)), DMA((2,)), DMA((2,)),
        DMA, DMA, DMA, DMA, DMA, DMA,
    ]
    shapes = (
        jax.ShapeDtypeStruct((patches, D), BF16),
        jax.ShapeDtypeStruct((S, D), F32),
        jax.ShapeDtypeStruct(weight_in.shape, BF16),
        jax.ShapeDtypeStruct(weight_out.shape, BF16),
    )
    results = pl.pallas_call(
        functools.partial(kernel, ZL, XY),
        out_shape=shapes,
        in_specs=[in_hbm] * 5,
        out_specs=[in_vmem, in_vmem, anywhere, anywhere],
        scratch_shapes=scratch,
        compiler_params=pltpu.CompilerParams(
            collective_id=0, has_side_effects=True, vmem_limit_bytes=40 * 1024 * 1024
        ),
    )(*(pltpu.with_memory_space_constraint(x, pltpu.HBM) for x in (tokens[0], slot_param.T, weight_in, weight_out, grad_out[0])))
    grad_tokens, grad_param, grad_win, grad_wout = pl.pallas_call(
        deliver,
        out_shape=shapes,
        in_specs=[anywhere] * 4,
        out_specs=[in_hbm] * 4,
        scratch_shapes=[DMA((18,))],
        compiler_params=pltpu.CompilerParams(vmem_limit_bytes=1024 * 1024),
    )(*results)
    return grad_tokens[None], grad_param.T, grad_win, grad_wout


def solution(mesh):
    ZL = mesh.shape["ex"] // 2
    XY = mesh.shape["ey"] // ZH
    split = Mesh(mesh.devices.reshape(ZL, 2, ZH, XY), AXES)
    return jax.shard_map(
        functools.partial(per_device, ZL, XY),
        mesh=split,
        in_specs=(P(ALL, None, None), P(), P(EY, None, EX), P(EY, EX, None), P(ALL, None, None)),
        out_specs=(P(ALL, None, None), P(), P(EY, None, EX), P(EY, EX, None)),
        check_vma=False,
    )
```
